32 devices in a mesh: src: 16 (over z, y, core), tgt: 2 (over x).
Axes of the slice: x: 2, y: 2, z: 4, core: 2. Of those that a mesh axis runs over, the one named last changes fastest.
Arguments:
- edge_states: bfloat16 [16, 2, 512, 1024], P('src', 'tgt'), may hold values from -6 to 6
- triplet_coeff: bfloat16 [16, 2, 16, 128, 128], P('src', 'tgt'), may hold values from -0.3984375 to 0.3984375
- block_target: int32 [16, 2, 16], P('src', 'tgt'), may hold values from 0 to 3
- block_source: int32 [16, 2, 16], P('src', 'tgt'), may hold values from 0 to 63
- block_count: int32 [16, 2], P('src', 'tgt'), may hold values from 2 to 16, as said below
- reverse_slot: int32 [16, 2, 512], P('src', 'tgt'), may hold values from 0 to 511, as said below
- w_proj: bfloat16 [2, 1024, 64], replicated, may hold values from -0.1875 to 0.1875
- w_up: bfloat16 [2, 64, 1024], replicated, may hold values from -0.75 to 0.75
- w_in: bfloat16 [2, 1024, 1024], replicated, may hold values from -0.1875 to 0.1875
- w_out: bfloat16 [2, 1024, 1024], replicated, may hold values from -0.1875 to 0.1875
- norm_gain: float32 [2, 1024], replicated, may hold values from 0.5 to 2
Outputs:
- edge_final: bfloat16 [16, 2, 512, 1024], P('src', 'tgt')
The draws below stay inside these ranges and needn't reach their ends.
Inputs may be any that keep to these rules, and one draw needn't show every extreme that they name: `block_count`: each tile uses between 2 and 16 blocks; some tile uses all 16 in every draw. Reverse edges pair up: with C = 8, for tile (p, q) with p = a * C + r and its mirror tile (q * C + r, a), the two reverse_slot rows are inverse permutations of 0 to 511; on a tile with a = q the row is a permutation that is its own inverse without fixed points.
All inputs are finite; a program needn't handle non-finite values.
Results may differ from the reference program's by a relative error of at most 0.014.
Values may be sent and summed in bfloat16 or wider, within the bound.
No kernel may reach another device: no remote copies, remote signals or barrier semaphores. Data moves between devices by JAX's collectives and lax.ppermute only.
A program may use at most 64 MiB of HBM per device.

```python
import math
import jax
import jax.numpy as jnp
from jax import lax

D = 1024
TRIP = 64
E_TILE = 512
BLK = 128
LAYERS = 2
NB = 16
N_SRC = 16
N_TGT = 2


def draw_block_count(key, part):
    key_base = jax.random.fold_in(key, 11)
    key_full = jax.random.fold_in(key, 12)
    key_pick = jax.random.fold_in(key, 13)
    lowest = max(1, NB // 8)
    base_counts = jax.random.randint(key_base, (N_SRC, N_TGT), lowest, NB // 2 + 1)
    full_tiles = jax.random.randint(key_full, (N_SRC, N_TGT), 0, 16) == 0
    counts = jnp.where(full_tiles, NB, base_counts).reshape(-1)
    chosen = jax.random.randint(key_pick, (), 0, N_SRC * N_TGT)
    counts = jnp.where(jnp.arange(N_SRC * N_TGT) == chosen, NB, counts)
    return counts.reshape(N_SRC, N_TGT).astype(jnp.int32)


def draw_reverse_slot(key, part):
    groups = N_TGT
    copies = N_SRC // groups
    tile_keys = jax.random.split(jax.random.fold_in(key, 21), copies * groups * groups)
    perms = jax.vmap(lambda single: jax.random.permutation(single, E_TILE))(tile_keys)
    perms = perms.reshape(copies, groups, groups, E_TILE).astype(jnp.int32)
    inverse = jnp.argsort(perms, axis=-1).astype(jnp.int32)
    partner = perms.reshape(copies, groups, groups, E_TILE // 2, 2)[..., ::-1].reshape(copies, groups, groups, E_TILE)
    involution = jnp.take_along_axis(partner, inverse, axis=-1)
    row_group = jnp.arange(groups)[None, :, None, None]
    col_group = jnp.arange(groups)[None, None, :, None]
    result = jnp.where(row_group < col_group, perms, jnp.where(row_group > col_group, inverse.swapaxes(1, 2), involution))
    result = result.transpose(1, 0, 2, 3)
    return result.reshape(N_SRC, N_TGT, E_TILE).astype(jnp.int32)


def touch_ends(values, stream_key, smallest, high):
    extent = values.shape
    spot = [jax.random.randint(jax.random.fold_in(stream_key, axis), (), 0, extent[axis]) for axis in range(len(extent))]
    values = values.at[tuple(spot)].set(smallest)
    longest = extent.index(max(extent))
    spot[longest] = (spot[longest] + 1) % extent[longest]
    return values.at[tuple(spot)].set(high)


def block_levels(rng, extent, cuts, smallest, largest):
    loudness = 1.0
    for position, blocks in cuts:
        draws = jax.random.uniform(jax.random.fold_in(jax.random.fold_in(rng, 6), position), (blocks,), jnp.float32, smallest / len(cuts), largest / len(cuts))
        loudness = loudness * jnp.repeat(jnp.exp(draws), extent[position] // blocks).reshape((-1,) + (1,) * (len(extent) - 1 - position))
    return loudness


def gaussian(rng, extent, width, bound, cuts=(), dtype=jnp.bfloat16):
    level = block_levels(rng, extent, cuts, -0.22, 0.18) if cuts else 1.0
    array = jax.random.normal(rng, extent, jnp.float32) * width * level
    return jnp.minimum(jnp.maximum(array, -bound), bound).astype(dtype)


def setup_inputs(seed: int = 0) -> dict:
    seeds = jax.random.split(jax.random.key(seed), 12)
    edge_states = gaussian(seeds[0], (N_SRC, N_TGT, E_TILE, D), 1.0, 6.0, ((0, 16), (1, 2)))
    triplet_coeff = gaussian(seeds[1], (N_SRC, N_TGT, NB, BLK, BLK), 0.05, 0.3984375, ((0, 16), (1, 2)))
    block_target = touch_ends(jax.random.randint(seeds[2], (N_SRC, N_TGT, NB), 0, E_TILE // BLK), jax.random.fold_in(seeds[2], 1), 0, (E_TILE // BLK) - 1).astype(jnp.int32)
    block_source = touch_ends(jax.random.randint(seeds[3], (N_SRC, N_TGT, NB), 0, N_SRC * E_TILE // BLK), jax.random.fold_in(seeds[3], 1), 0, (N_SRC * E_TILE // BLK) - 1).astype(jnp.int32)
    block_count = draw_block_count(jax.random.fold_in(seeds[11], 71), 0)
    reverse_slot = draw_reverse_slot(jax.random.fold_in(seeds[11], 71), 0)
    w_proj = gaussian(seeds[6], (LAYERS, D, TRIP), D ** -0.5, 0.1875)
    w_up = gaussian(seeds[7], (LAYERS, TRIP, D), TRIP ** -0.5, 0.75)
    w_in = gaussian(seeds[8], (LAYERS, D, D), D ** -0.5, 0.1875)
    w_out = gaussian(seeds[9], (LAYERS, D, D), D ** -0.5, 0.1875)
    norm_gain = jnp.clip(jnp.exp(jax.random.uniform(seeds[10], (LAYERS, D), jnp.float32, math.log(0.5), math.log(2.0))), 0.5, 2.0)
    return dict(edge_states=edge_states, triplet_coeff=triplet_coeff, block_target=block_target, block_source=block_source, block_count=block_count, reverse_slot=reverse_slot, w_proj=w_proj, w_up=w_up, w_in=w_in, w_out=w_out, norm_gain=norm_gain)


def mirror_of(values, reverse_slot):
    groups = N_TGT
    copies = N_SRC // groups
    turned = values.reshape((groups, copies, groups) + values.shape[2:]).swapaxes(0, 2).reshape(values.shape)
    return jnp.take_along_axis(turned, reverse_slot[..., None], axis=2)

def reference(edge_states, triplet_coeff, block_target, block_source, block_count, reverse_slot, w_proj, w_up, w_in, w_out, norm_gain):
    out_blocks = E_TILE // BLK
    live_mask = (jnp.arange(NB)[None, None, :] < block_count[:, :, None]).astype(jnp.float32)
    placing = (block_target[..., None] == jnp.arange(out_blocks)[None, None, None, :]).astype(jnp.float32) * live_mask[..., None]
    coeffs = triplet_coeff.astype(jnp.float32)
    state = edge_states
    for layer_index in range(LAYERS):
        proj = jnp.einsum('sted,dc->stec', state.astype(jnp.float32), w_proj[layer_index].astype(jnp.float32)).astype(jnp.bfloat16)
        pooled = proj.swapaxes(0, 1).reshape(N_TGT, N_SRC * out_blocks, BLK, TRIP)
        picked = pooled[jnp.arange(N_TGT)[None, :, None], block_source]
        products = jnp.einsum('stbji,stbjc->stbic', coeffs, picked.astype(jnp.float32))
        agg = jnp.einsum('stbic,stbo->stoic', products, placing).reshape(N_SRC, N_TGT, E_TILE, TRIP).astype(jnp.bfloat16)
        summed = state.astype(jnp.float32) + jnp.einsum('stec,cd->sted', agg.astype(jnp.float32), w_up[layer_index].astype(jnp.float32))
        scale_inv = lax.rsqrt(lax.optimization_barrier(jnp.mean(summed * summed, axis=-1, keepdims=True)) + 1e-06)
        normed = (norm_gain[layer_index] * summed * scale_inv).astype(jnp.bfloat16)
        activated = jax.nn.silu(jnp.einsum('sted,dh->steh', normed.astype(jnp.float32), w_in[layer_index].astype(jnp.float32))).astype(jnp.bfloat16)
        branch = jnp.einsum('steh,hd->sted', activated.astype(jnp.float32), w_out[layer_index].astype(jnp.float32)).astype(jnp.bfloat16)
        state = (summed + branch.astype(jnp.float32) + mirror_of(branch, reverse_slot).astype(jnp.float32)).astype(jnp.bfloat16)
    return state
```

```python
import jax
import jax.numpy as jnp
from jax import lax
from jax.sharding import PartitionSpec as P

BLK = 128
LAYERS = 2


def mirror_pairs():
    groups = lax.axis_size("tgt")
    copies = lax.axis_size("src") // groups
    pairs = []
    for p in range(groups * copies):
        a, r = divmod(p, copies)
        for q in range(groups):
            if a != q:
                pairs.append((p * groups + q, (q * copies + r) * groups + a))
    return pairs


def mirror_tile(values):
    copies = lax.axis_size("src") // lax.axis_size("tgt")
    same = lax.axis_index("src") // copies == lax.axis_index("tgt")
    moved = lax.ppermute(values, ("src", "tgt"), mirror_pairs())
    return jnp.where(same, values, moved)


def gather_pool(projected):
    size = lax.axis_size("src")
    held = projected[None]
    bit = size // 2
    while bit:
        held = jnp.concatenate(
            [held, lax.ppermute(held, "src", [(i, i ^ bit) for i in range(size)])], axis=0
        )
        bit //= 2
    return held


def pool_slots(sources, blocks_per_tile):
    size = lax.axis_size("src")
    relative = (sources // blocks_per_tile) ^ lax.axis_index("src")
    slots = jnp.zeros_like(relative)
    bit, place = size // 2, 1
    while bit:
        slots = slots + jnp.where((relative & bit) != 0, place, 0)
        bit //= 2
        place *= 2
    return slots, sources % blocks_per_tile


def triplet_sums(pooled, coeffs, targets, sources, live_count, edge_count):
    width = pooled.shape[1]
    slots = coeffs.shape[0]
    out_blocks = edge_count // BLK
    tile, block = pool_slots(sources, out_blocks)
    picked = jnp.stack(
        [
            lax.dynamic_slice(pooled, (tile[b], 0, block[b] * BLK), (1, width, BLK))[0]
            for b in range(slots)
        ],
        axis=1,
    )
    products = jnp.einsum("cbj,bji->cbi", picked, coeffs, preferred_element_type=jnp.float32)
    live_mask = (jnp.arange(slots) < live_count).astype(jnp.float32)
    placing = (targets[:, None] == jnp.arange(out_blocks)[None, :]).astype(jnp.float32) * live_mask[
        :, None
    ]
    return jnp.einsum("cbi,bo->coi", products, placing).reshape(width, edge_count)


def transform(rows, agg_low, w_up_l, w_in_l, w_out_l, gain_l):
    summed = rows.astype(jnp.float32) + jnp.einsum(
        "ce,cd->ed", agg_low, w_up_l, preferred_element_type=jnp.float32
    )
    scale_inv = lax.rsqrt(jnp.mean(summed * summed, axis=-1, keepdims=True) + 1e-06)
    normed = (gain_l * summed * scale_inv).astype(jnp.bfloat16)
    activated = jax.nn.silu(jnp.dot(normed, w_in_l, preferred_element_type=jnp.float32)).astype(
        jnp.bfloat16
    )
    branch = jnp.dot(activated, w_out_l, preferred_element_type=jnp.float32).astype(jnp.bfloat16)
    return (summed, branch)


def local(
    edge_states,
    triplet_coeff,
    block_target,
    block_source,
    block_count,
    reverse_slot,
    w_proj,
    w_up,
    w_in,
    w_out,
    norm_gain,
):
    state = edge_states[0, 0]
    coeffs = triplet_coeff[0, 0]
    targets = block_target[0, 0]
    sources = block_source[0, 0]
    live_count = block_count[0, 0]
    reverse_rows = reverse_slot[0, 0]
    edge_count = state.shape[0]
    mirrored = jnp.take(mirror_tile(state), reverse_rows, axis=0)
    for layer_index in range(LAYERS):
        projected = jnp.einsum(
            "ed,dc->ce", state, w_proj[layer_index], preferred_element_type=jnp.float32
        ).astype(jnp.bfloat16)
        pooled = gather_pool(projected)
        agg_low = triplet_sums(pooled, coeffs, targets, sources, live_count, edge_count).astype(
            jnp.bfloat16
        )
        summed, branch = transform(
            state,
            agg_low,
            w_up[layer_index],
            w_in[layer_index],
            w_out[layer_index],
            norm_gain[layer_index],
        )
        agg_mirror = jnp.take(mirror_tile(agg_low), reverse_rows, axis=1)
        summed_mirror, branch_mirror = transform(
            mirrored,
            agg_mirror,
            w_up[layer_index],
            w_in[layer_index],
            w_out[layer_index],
            norm_gain[layer_index],
        )
        state = (summed + branch.astype(jnp.float32) + branch_mirror.astype(jnp.float32)).astype(
            jnp.bfloat16
        )
        mirrored = (
            summed_mirror + branch_mirror.astype(jnp.float32) + branch.astype(jnp.float32)
        ).astype(jnp.bfloat16)
    return state[None, None]


def solution(mesh):
    return jax.shard_map(
        local,
        mesh=mesh,
        in_specs=(
            P("src", "tgt", None, None),
            P("src", "tgt", None, None, None),
            P("src", "tgt", None),
            P("src", "tgt", None),
            P("src", "tgt"),
            P("src", "tgt", None),
            P(),
            P(),
            P(),
            P(),
            P(),
        ),
        out_specs=P("src", "tgt", None, None),
        check_vma=False,
    )
```

```python
import functools

import jax
import jax.numpy as jnp
from jax import lax
from jax.experimental import pallas as pl
from jax.experimental.pallas import tpu as pltpu
from jax.sharding import PartitionSpec as P

BLK = 128
LAYERS = 2
ROWS = 256
EXCHANGE_BITS = 2
VMEM_LIMIT = 24 * 2**20
F32 = jnp.float32
BF16 = jnp.bfloat16


def dot(x, y):
    return jnp.dot(x, y, preferred_element_type=F32)


def dot_nt(x, y):
    return lax.dot_general(x, y, (((1,), (1,)), ((), ())), preferred_element_type=F32)


def reversed_bits(value, bits):
    return sum((value >> i & 1) << bits - 1 - i for i in range(bits))


def hop(values, bit):
    size = lax.axis_size("src")
    return lax.ppermute(values, "src", [(i, i ^ bit) for i in range(size)])


def mirror_pairs():
    groups = lax.axis_size("tgt")
    copies = lax.axis_size("src") // groups
    pairs = []
    for p in range(groups * copies):
        a, r = divmod(p, copies)
        for q in range(groups):
            if a != q:
                pairs.append((p * groups + q, (q * copies + r) * groups + a))
    return pairs


def to_mirror(values):
    return lax.ppermute(values, ("src", "tgt"), mirror_pairs())


def call(body, name, outs, scalars, arrays, scratch=(), flops=0, moved=0):
    smem = pl.BlockSpec(memory_space=pltpu.SMEM)
    vmem = pl.BlockSpec(memory_space=pltpu.VMEM)
    return pl.pallas_call(
        body,
        in_specs=[smem] * len(scalars) + [vmem] * len(arrays),
        out_specs=[vmem] * len(outs),
        scratch_shapes=list(scratch),
        out_shape=list(outs),
        name=name,
        compiler_params=pltpu.CompilerParams(vmem_limit_bytes=VMEM_LIMIT),
        cost_estimate=pl.CostEstimate(flops=flops, bytes_accessed=moved, transcendentals=0),
    )(*scalars, *arrays)


def reverse_column(reverse_row):
    return jnp.broadcast_to(reverse_row[...], (8, reverse_row.shape[1])).T[:, :1]


def own_mirror():
    copies = lax.axis_size("src") // lax.axis_size("tgt")
    return lax.axis_index("src") // copies == lax.axis_index("tgt")


def like(shape, dtype):
    return jax.ShapeDtypeStruct(shape, dtype)


def project_body(w_proj_t, state, out):
    out[...] = dot_nt(w_proj_t[0], state[...]).astype(BF16)


def project(w_proj_t, state):
    shape = (w_proj_t.shape[1], state.shape[0])
    return call(
        project_body,
        "project",
        [like(shape, BF16)],
        [],
        [w_proj_t, state],
        flops=2 * state.size * shape[0],
        moved=2 * state.size,
    )[0]


def triplet_body(low_bits, slots, blocks, index, pool, coeffs, kept, sent, acc):
    acc[...] = jnp.zeros_like(acc)
    mine = lax.axis_index("src")
    low_mask = (1 << low_bits) - 1
    for tile in range(1 << low_bits):
        at = reversed_bits(tile, low_bits)

        def one(slot, carry):
            source = index[at, slots + slot]
            relative = (source // blocks) ^ mine

            @pl.when((relative & low_mask) == 0)
            def _():
                held_tile = jnp.int32(0)
                high = pool.shape[0]
                place, bit = 1, (high // 2) << low_bits
                while place < high:
                    held_tile = held_tile + jnp.where((relative & bit) != 0, place, 0)
                    place, bit = place * 2, bit // 2
                start = pl.multiple_of((source % blocks) * BLK, BLK)
                picked = pool[held_tile, :, pl.ds(start, BLK)]
                product = dot(picked, coeffs[at, slot])
                place_at = pl.multiple_of(index[at, slot] * BLK, BLK)
                acc[tile, :, pl.ds(place_at, BLK)] += product

            return carry

        lax.fori_loop(0, jnp.minimum(index[at, 2 * slots], slots), one, 0)
    half = acc.shape[0] // 2
    kept[...] = acc[:half]
    sent[...] = acc[half:].astype(BF16)


def triplet_partials(index, pool, coeffs):
    tiles, slots = coeffs.shape[:2]
    width, edges = pool.shape[1:]
    body = functools.partial(triplet_body, tiles.bit_length() - 1, slots, edges // BLK)
    return call(
        body,
        "triplets",
        [
            like((tiles // 2, width, edges), F32),
            like((tiles // 2, width, edges), BF16),
        ],
        [index],
        [pool, coeffs],
        scratch=[pltpu.VMEM((tiles, width, edges), F32)],
        flops=2 * coeffs.size * width,
        moved=2 * coeffs.size,
    )


def branch_of(x, agg, w_up, w_in, w_out, gain):
    summed = x.astype(F32) + dot(agg, w_up[...])
    scale_inv = lax.rsqrt(jnp.mean(summed * summed, axis=-1, keepdims=True) + 1e-06)
    normed = (gain[...] * summed * scale_inv).astype(BF16)
    u = dot(normed, w_in[...])
    activated = (u / (1.0 + jnp.exp(-u))).astype(BF16)
    return summed, dot(activated, w_out[...]).astype(BF16)


def chunks(edges):
    step = min(ROWS, edges)
    return [pl.ds(i, step) for i in range(0, edges, step)]


def weights_of(layer_index, w_up, w_in, w_out, gain):
    return [w.at[layer_index] for w in (w_up, w_in, w_out)] + [gain.at[pl.ds(layer_index, 1)]]


def one_hot(column):
    lanes = lax.broadcasted_iota(jnp.int32, (column.shape[0], column.shape[0]), 1)
    return (column == lanes).astype(BF16)


def picking(column, rows, edges):
    lanes = lax.broadcasted_iota(jnp.int32, (rows.size, edges), 1)
    return (column[rows.start : rows.start + rows.size] == lanes).astype(BF16)


def first_body(w_up, w_in, w_out, gain, w_proj_t, state, agg_t, reverse, total, branch, v_t, u_t):
    weights = weights_of(0, w_up, w_in, w_out, gain)
    agg = agg_t[...].astype(F32).T.astype(BF16)
    w_next = w_proj_t[1]
    for rows in chunks(state.shape[0]):
        summed, out = branch_of(state[rows, :], agg[rows.start : rows.start + rows.size], *weights)
        branch[rows, :] = out
        moved = summed + out.astype(F32)
        total[rows, :] = moved
        v_t[:, rows] = dot_nt(w_next, moved.astype(BF16)).astype(BF16)
    u = dot_nt(w_next, branch[...]).astype(BF16)
    u_t[...] = dot(u, one_hot(reverse_column(reverse))).astype(BF16)


def second_body(
    w_up, w_in, w_out, gain, own, other_low, other_high, agg_t, agg_other, reverse, total, branch, state, mirrored
):
    edges = total.shape[0]
    weights = weights_of(0, w_up, w_in, w_out, gain)
    here = own_mirror()
    other = jnp.concatenate([other_low[...], other_high[...]], axis=0)
    source = jnp.where(here, own[...], other)
    low = jnp.where(here, agg_t[...], agg_other[...])
    column = reverse_column(reverse)
    for rows in chunks(edges):
        pick = picking(column, rows, edges)
        summed, out = branch_of(dot(pick, source), dot_nt(pick, low).astype(BF16), *weights)
        state[rows, :] = (total[rows, :] + out.astype(F32)).astype(BF16)
        mirrored[rows, :] = (summed + out.astype(F32) + branch[rows, :].astype(F32)).astype(BF16)


def third_body(w_up, w_in, w_out, gain, state, agg_t, total):
    weights = weights_of(1, w_up, w_in, w_out, gain)
    agg = agg_t[...].astype(F32).T.astype(BF16)
    for rows in chunks(state.shape[0]):
        summed, out = branch_of(state[rows, :], agg[rows.start : rows.start + rows.size], *weights)
        total[rows, :] = summed + out.astype(F32)


def last_body(w_up, w_in, w_out, gain, mirrored, agg_t, agg_other, reverse, total, state):
    edges = total.shape[0]
    weights = weights_of(1, w_up, w_in, w_out, gain)
    low = jnp.where(own_mirror(), agg_t[...], agg_other[...])
    column = reverse_column(reverse)
    for rows in chunks(edges):
        agg = dot_nt(picking(column, rows, edges), low).astype(BF16)
        summed, out = branch_of(mirrored[rows, :], agg, *weights)
        state[rows, :] = (total[rows, :] + out.astype(F32)).astype(BF16)


def gather_step(held, bit):
    return jnp.concatenate([held, hop(held, bit)], axis=0)


def gather_low(values):
    held = values[None]
    for bit in reversed(range(EXCHANGE_BITS)):
        held = gather_step(held, 1 << bit)
    return held


def second_route_x(values):
    groups, size = lax.axis_size("tgt"), lax.axis_size("src")
    if groups != 2:
        return values
    copies = size // groups
    pairs = [
        ((a * copies + r) * 2 + 1 - a, (a * copies + r) * 2 + a)
        for a in range(2)
        for r in range(copies)
    ]
    return lax.ppermute(values, ("src", "tgt"), pairs)


def second_route_z(turned, values):
    groups, size = lax.axis_size("tgt"), lax.axis_size("src")
    if groups != 2:
        return to_mirror(values)
    copies = size // groups
    pairs = [
        ((a * copies + r) * 2 + a, ((1 - a) * copies + r) * 2 + a)
        for a in range(2)
        for r in range(copies)
    ]
    return lax.ppermute(turned, ("src", "tgt"), pairs)


def gather_high(projected):
    size = lax.axis_size("src")
    held = projected[None]
    bit = size // 2
    while bit >= 1 << EXCHANGE_BITS:
        held = jnp.concatenate([held, hop(held, bit)], axis=0)
        bit //= 2
    return held


def exchange_sums(kept, sent):
    bit = 1 << (EXCHANGE_BITS - 1)
    while True:
        summed = kept + hop(sent, bit).astype(F32)
        half = summed.shape[0] // 2
        if half == 0:
            return summed[0].astype(BF16)
        kept, sent = summed[:half], summed[half:].astype(BF16)
        bit //= 2


def local(
    edge_states,
    triplet_coeff,
    block_target,
    block_source,
    block_count,
    reverse_slot,
    w_proj,
    w_up,
    w_in,
    w_out,
    norm_gain,
):
    state0 = edge_states[0, 0]
    edges, features = state0.shape
    width = w_proj.shape[2]
    reverse = reverse_slot[0]
    w_proj_t = jnp.swapaxes(w_proj, 1, 2)
    weights = [w_up, w_in, w_out, norm_gain]

    proj0 = project(w_proj_t, state0)
    own_index = jnp.concatenate([block_target[0, 0], block_source[0, 0], block_count[0]])
    own_coeffs, own_index, held_state, proj0 = lax.optimization_barrier(
        (triplet_coeff[0, 0], own_index, state0, proj0)
    )
    index = gather_low(own_index)
    half = edges // 2
    turned = second_route_x(held_state[half:])
    coeffs_y = gather_step(own_coeffs[None], 1 << (EXCHANGE_BITS - 1))
    pool = gather_high(proj0)
    coeffs_y, held_state, turned, pool = lax.optimization_barrier(
        (coeffs_y, held_state, turned, pool)
    )
    coeffs = gather_step(coeffs_y, 1)
    other_low = to_mirror(held_state[:half])
    other_high = second_route_z(turned, held_state[half:])
    kept, sent = triplet_partials(index, pool, coeffs)
    agg0 = exchange_sums(kept, sent)
    work = 4 * edges * features * features
    total0, branch0, v_t, u_t = call(
        first_body,
        "first",
        [
            like((edges, features), F32),
            like((edges, features), BF16),
            like((width, edges), BF16),
            like((width, edges), BF16),
        ],
        [],
        weights + [w_proj_t, state0, agg0, reverse],
        flops=work,
        moved=8 * 2**20,
    )
    u_t, other_low, other_high = lax.optimization_barrier((u_t, other_low, other_high))
    u_other = to_mirror(u_t)
    agg0_other = to_mirror(agg0)
    mirrored_u = jnp.where(own_mirror(), u_t, u_other)
    proj1 = (v_t.astype(F32) + mirrored_u.astype(F32)).astype(BF16)
    pool1 = gather_high(proj1)
    kept, sent = triplet_partials(index, pool1, coeffs)
    agg1 = exchange_sums(kept, sent)
    agg1_other = to_mirror(agg1)
    state1, mirrored1 = call(
        second_body,
        "second",
        [like((edges, features), BF16), like((edges, features), BF16)],
        [],
        weights + [state0, other_low, other_high, agg0, agg0_other, reverse, total0, branch0],
        flops=work + 2 * edges * edges * features,
        moved=10 * 2**20,
    )
    total1 = call(
        third_body,
        "third",
        [like((edges, features), F32)],
        [],
        weights + [state1, agg1],
        flops=work,
        moved=8 * 2**20,
    )[0]
    final = call(
        last_body,
        "last",
        [like((edges, features), BF16)],
        [],
        weights + [mirrored1, agg1, agg1_other, reverse, total1],
        flops=work,
        moved=8 * 2**20,
    )[0]
    return final[None, None]


def solution(mesh):
    return jax.shard_map(
        local,
        mesh=mesh,
        in_specs=(
            P("src", "tgt", None, None),
            P("src", "tgt", None, None, None),
            P("src", "tgt", None),
            P("src", "tgt", None),
            P("src", "tgt"),
            P("src", "tgt", None),
            P(),
            P(),
            P(),
            P(),
            P(),
        ),
        out_specs=P("src", "tgt", None, None),
        check_vma=False,
    )
```

```python
import functools

import jax
import jax.numpy as jnp
from jax import lax
from jax.experimental import pallas as pl
from jax.experimental.pallas import tpu as pltpu
from jax.sharding import PartitionSpec as P

BLK = 128
LAYERS = 2
ROWS = 256
EXCHANGE_BITS = 2
MIB = 2**20
F32 = jnp.float32
BF16 = jnp.bfloat16


def dot(x, y):
    return jnp.dot(x, y, preferred_element_type=F32)


def dot_nt(x, y):
    return lax.dot_general(x, y, (((1,), (1,)), ((), ())), preferred_element_type=F32)


def reversed_bits(value, bits):
    return sum((value >> i & 1) << bits - 1 - i for i in range(bits))


def hop(values, bit):
    size = lax.axis_size("src")
    return lax.ppermute(values, "src", [(i, i ^ bit) for i in range(size)])


def mirror_pairs():
    groups = lax.axis_size("tgt")
    copies = lax.axis_size("src") // groups
    pairs = []
    for p in range(groups * copies):
        a, r = divmod(p, copies)
        for q in range(groups):
            if a != q:
                pairs.append((p * groups + q, (q * copies + r) * groups + a))
    return pairs


def to_mirror(values):
    return lax.ppermute(values, ("src", "tgt"), mirror_pairs())


def call(body, name, outs, scalars, arrays, scratch=(), flops=0, moved=0, limit=18):
    smem = pl.BlockSpec(memory_space=pltpu.SMEM)
    vmem = pl.BlockSpec(memory_space=pltpu.VMEM)
    return pl.pallas_call(
        body,
        in_specs=[smem] * len(scalars) + [vmem] * len(arrays),
        out_specs=[vmem] * len(outs),
        scratch_shapes=list(scratch),
        out_shape=list(outs),
        name=name,
        compiler_params=pltpu.CompilerParams(vmem_limit_bytes=limit * MIB),
        cost_estimate=pl.CostEstimate(flops=flops, bytes_accessed=moved, transcendentals=0),
    )(*scalars, *arrays)


def reverse_column(reverse_row):
    return jnp.broadcast_to(reverse_row[...], (8, reverse_row.shape[1])).T[:, :1]


def own_mirror():
    copies = lax.axis_size("src") // lax.axis_size("tgt")
    return lax.axis_index("src") // copies == lax.axis_index("tgt")


def like(shape, dtype):
    return jax.ShapeDtypeStruct(shape, dtype)


def project_body(w_proj_t, state, out):
    out[...] = dot_nt(w_proj_t[0], state[...]).astype(BF16)


def project(w_proj_t, state):
    shape = (w_proj_t.shape[1], state.shape[0])
    return call(
        project_body,
        "project",
        [like(shape, BF16)],
        [],
        [w_proj_t, state],
        flops=2 * state.size * shape[0],
        moved=2 * state.size,
        limit=8,
    )[0]


def triplet_body(low_bits, slots, blocks, index, pool, coeffs, kept, sent, acc):
    acc[...] = jnp.zeros_like(acc)
    mine = lax.axis_index("src")
    low_mask = (1 << low_bits) - 1
    for tile in range(1 << low_bits):
        at = reversed_bits(tile, low_bits)

        def one(slot, carry):
            source = index[at, slots + slot]
            relative = (source // blocks) ^ mine

            @pl.when((relative & low_mask) == 0)
            def _():
                held_tile = jnp.int32(0)
                high = pool.shape[0]
                place, bit = 1, (high // 2) << low_bits
                while place < high:
                    held_tile = held_tile + jnp.where((relative & bit) != 0, place, 0)
                    place, bit = place * 2, bit // 2
                start = pl.multiple_of((source % blocks) * BLK, BLK)
                picked = pool[held_tile, :, pl.ds(start, BLK)]
                product = dot(picked, coeffs[at, slot])
                place_at = pl.multiple_of(index[at, slot] * BLK, BLK)
                acc[tile, :, pl.ds(place_at, BLK)] += product

            return carry

        lax.fori_loop(0, jnp.minimum(index[at, 2 * slots], slots), one, 0)
    half = acc.shape[0] // 2
    kept[...] = acc[:half]
    sent[...] = acc[half:].astype(BF16)


def triplet_partials(index, pool, coeffs):
    tiles, slots = coeffs.shape[:2]
    width, edges = pool.shape[1:]
    body = functools.partial(triplet_body, tiles.bit_length() - 1, slots, edges // BLK)
    return call(
        body,
        "triplets",
        [
            like((tiles // 2, width, edges), F32),
            like((tiles // 2, width, edges), BF16),
        ],
        [index],
        [pool, coeffs],
        scratch=[pltpu.VMEM((tiles, width, edges), F32)],
        flops=2 * coeffs.size * width,
        moved=2 * coeffs.size,
        limit=8,
    )


def branch_of(x, agg, w_up, w_in, w_out, gain):
    summed = x.astype(F32) + dot(agg, w_up[...])
    scale_inv = lax.rsqrt(jnp.mean(summed * summed, axis=-1, keepdims=True) + 1e-06)
    normed = (gain[...] * summed * scale_inv).astype(BF16)
    u = dot(normed, w_in[...])
    activated = (u / (1.0 + jnp.exp(-u))).astype(BF16)
    return summed, dot(activated, w_out[...]).astype(BF16)


def chunks(edges):
    step = min(ROWS, edges)
    return [pl.ds(i, step) for i in range(0, edges, step)]


def weights_of(layer_index, w_up, w_in, w_out, gain):
    return [w.at[layer_index] for w in (w_up, w_in, w_out)] + [gain.at[pl.ds(layer_index, 1)]]


def picking(column, rows, edges):
    lanes = lax.broadcasted_iota(jnp.int32, (rows.size, edges), 1)
    return (column[rows.start : rows.start + rows.size] == lanes).astype(BF16)


def first_body(w_up, w_in, w_out, gain, w_proj_t, state, agg_t, reverse, total, branch, v_t, u_t):
    weights = weights_of(0, w_up, w_in, w_out, gain)
    agg = agg_t[...].astype(F32).T.astype(BF16)
    w_next = w_proj_t[1]
    for rows in chunks(state.shape[0]):
        summed, out = branch_of(state[rows, :], agg[rows.start : rows.start + rows.size], *weights)
        branch[rows, :] = out
        moved = summed + out.astype(F32)
        total[rows, :] = moved
        v_t[:, rows] = dot_nt(w_next, moved.astype(BF16)).astype(BF16)
    u = dot_nt(w_next, branch[...]).astype(BF16)
    edges = u.shape[1]
    rows = lax.broadcasted_iota(jnp.int32, (edges, edges), 0)
    u_t[...] = dot_nt(u, (reverse[...] == rows).astype(BF16)).astype(BF16)


def combine_body(v_t, u_t, u_other, out):
    mirrored = jnp.where(own_mirror(), u_t[...], u_other[...])
    out[...] = (v_t[...].astype(F32) + mirrored.astype(F32)).astype(BF16)


def second_body(
    w_up, w_in, w_out, gain, own, other_low, other_high, agg_t, agg_other, reverse, total, branch, state, mirrored
):
    edges = total.shape[0]
    weights = weights_of(0, w_up, w_in, w_out, gain)
    here = own_mirror()
    other = jnp.concatenate([other_low[...], other_high[...]], axis=0)
    source = jnp.where(here, own[...], other)
    low = jnp.where(here, agg_t[...], agg_other[...])
    column = reverse_column(reverse)
    for rows in chunks(edges):
        pick = picking(column, rows, edges)
        summed, out = branch_of(dot(pick, source), dot_nt(pick, low).astype(BF16), *weights)
        state[rows, :] = (total[rows, :] + out.astype(F32)).astype(BF16)
        mirrored[rows, :] = (summed + out.astype(F32) + branch[rows, :].astype(F32)).astype(BF16)


def third_body(w_up, w_in, w_out, gain, state, agg_t, total):
    weights = weights_of(1, w_up, w_in, w_out, gain)
    agg = agg_t[...].astype(F32).T.astype(BF16)
    for rows in chunks(state.shape[0]):
        summed, out = branch_of(state[rows, :], agg[rows.start : rows.start + rows.size], *weights)
        total[rows, :] = summed + out.astype(F32)


def last_body(w_up, w_in, w_out, gain, mirrored, agg_t, agg_other, reverse, total, state):
    edges = total.shape[0]
    weights = weights_of(1, w_up, w_in, w_out, gain)
    low = jnp.where(own_mirror(), agg_t[...], agg_other[...])
    at = lax.broadcasted_iota(jnp.int32, (edges, edges), 0)
    agg = dot(low, (reverse[...] == at).astype(BF16)).T.astype(BF16)
    for rows in chunks(edges):
        summed, out = branch_of(
            mirrored[rows, :], agg[rows.start : rows.start + rows.size], *weights
        )
        state[rows, :] = (total[rows, :] + out.astype(F32)).astype(BF16)


def gather_step(held, bit):
    return jnp.concatenate([held, hop(held, bit)], axis=0)


def gather_low(values):
    held = values[None]
    for bit in reversed(range(EXCHANGE_BITS)):
        held = gather_step(held, 1 << bit)
    return held


def second_route_x(values):
    groups, size = lax.axis_size("tgt"), lax.axis_size("src")
    if groups != 2:
        return values
    copies = size // groups
    pairs = [
        ((a * copies + r) * 2 + 1 - a, (a * copies + r) * 2 + a)
        for a in range(2)
        for r in range(copies)
    ]
    return lax.ppermute(values, ("src", "tgt"), pairs)


def second_route_z(turned, values):
    groups, size = lax.axis_size("tgt"), lax.axis_size("src")
    if groups != 2:
        return to_mirror(values)
    copies = size // groups
    pairs = [
        ((a * copies + r) * 2 + a, ((1 - a) * copies + r) * 2 + a)
        for a in range(2)
        for r in range(copies)
    ]
    return lax.ppermute(turned, ("src", "tgt"), pairs)


def gather_high(projected):
    size = lax.axis_size("src")
    held = projected[None]
    bit = size // 2
    while bit >= 1 << EXCHANGE_BITS:
        held = jnp.concatenate([held, hop(held, bit)], axis=0)
        bit //= 2
    return held


def exchange_sums(kept, sent):
    bit = 1 << (EXCHANGE_BITS - 1)
    while True:
        summed = kept + hop(sent, bit).astype(F32)
        half = summed.shape[0] // 2
        if half == 0:
            return summed[0].astype(BF16)
        kept, sent = summed[:half], summed[half:].astype(BF16)
        bit //= 2


def local(
    edge_states,
    triplet_coeff,
    block_target,
    block_source,
    block_count,
    reverse_slot,
    w_proj,
    w_up,
    w_in,
    w_out,
    norm_gain,
):
    state0 = edge_states[0, 0]
    edges, features = state0.shape
    width = w_proj.shape[2]
    reverse = reverse_slot[0]
    w_proj_t = jnp.swapaxes(w_proj, 1, 2)
    weights = [w_up, w_in, w_out, norm_gain]

    high, low = 1 << (EXCHANGE_BITS - 1), 1
    own_index = jnp.concatenate([block_target[0, 0], block_source[0, 0], block_count[0]])
    index_y = gather_step(own_index[None], high)
    index_y, state_in = lax.optimization_barrier((index_y, state0))
    proj0 = project(w_proj_t, state_in)
    index_y, own_coeffs, held_state, proj0 = lax.optimization_barrier(
        (index_y, triplet_coeff[0, 0], state0, proj0)
    )
    half = edges // 2
    turned = second_route_x(held_state[half:])
    coeffs_y = gather_step(own_coeffs[None], high)
    index = gather_step(index_y, low)
    pool = gather_high(proj0)
    index, coeffs_y, held_state, turned, pool = lax.optimization_barrier(
        (index, coeffs_y, held_state, turned, pool)
    )
    coeffs = gather_step(coeffs_y, low)
    other_low = to_mirror(held_state[:half])
    other_high = second_route_z(turned, held_state[half:])
    kept, sent = triplet_partials(index, pool, coeffs)
    agg0 = exchange_sums(kept, sent)
    work = 4 * edges * features * features
    total0, branch0, v_t, u_t = call(
        first_body,
        "first",
        [
            like((edges, features), F32),
            like((edges, features), BF16),
            like((width, edges), BF16),
            like((width, edges), BF16),
        ],
        [],
        weights + [w_proj_t, state0, agg0, reverse],
        flops=work,
        moved=8 * 2**20,
    )
    agg0_other = to_mirror(agg0)
    u_t, other_low, other_high, agg0_other = lax.optimization_barrier(
        (u_t, other_low, other_high, agg0_other)
    )
    u_other = to_mirror(u_t)
    proj1 = call(combine_body, "combine", [like(u_t.shape, BF16)], [], [v_t, u_t, u_other], limit=4)[0]
    pool1 = gather_high(proj1)
    state1, mirrored1 = call(
        second_body,
        "second",
        [like((edges, features), BF16), like((edges, features), BF16)],
        [],
        weights + [state0, other_low, other_high, agg0, agg0_other, reverse, total0, branch0],
        flops=work + 2 * edges * edges * features,
        moved=10 * 2**20,
    )
    state1, mirrored1, pool1 = lax.optimization_barrier((state1, mirrored1, pool1))
    kept, sent = triplet_partials(index, pool1, coeffs)
    agg1 = exchange_sums(kept, sent)
    agg1_other = to_mirror(agg1)
    total1 = call(
        third_body,
        "third",
        [like((edges, features), F32)],
        [],
        weights + [state1, agg1],
        flops=work,
        moved=8 * 2**20,
    )[0]
    final = call(
        last_body,
        "last",
        [like((edges, features), BF16)],
        [],
        weights + [mirrored1, agg1, agg1_other, reverse, total1],
        flops=work,
        moved=8 * 2**20,
    )[0]
    return final[None, None]


def solution(mesh):
    return jax.shard_map(
        local,
        mesh=mesh,
        in_specs=(
            P("src", "tgt", None, None),
            P("src", "tgt", None, None, None),
            P("src", "tgt", None),
            P("src", "tgt", None),
            P("src", "tgt"),
            P("src", "tgt", None),
            P(),
            P(),
            P(),
            P(),
            P(),
        ),
        out_specs=P("src", "tgt", None, None),
        check_vma=False,
    )
```

```python
import functools

import jax
import jax.numpy as jnp
from jax import lax
from jax.experimental import pallas as pl
from jax.experimental.pallas import tpu as pltpu
from jax.sharding import PartitionSpec as P

BLK = 128
LAYERS = 2
ROWS = 256
EARLY = 12
PROJECT_FLOPS = 10 * 1153 * 10**6
MIB = 2**20
F32 = jnp.float32
BF16 = jnp.bfloat16


def dot(x, y):
    return jnp.dot(x, y, preferred_element_type=F32)


def dot_nt(x, y):
    return lax.dot_general(x, y, (((1,), (1,)), ((), ())), preferred_element_type=F32)


def hop(values, bit):
    size = lax.axis_size("src")
    return lax.ppermute(values, "src", [(i, i ^ bit) for i in range(size)])


def mirror_pairs():
    groups = lax.axis_size("tgt")
    copies = lax.axis_size("src") // groups
    pairs = []
    for p in range(groups * copies):
        a, r = divmod(p, copies)
        for q in range(groups):
            if a != q:
                pairs.append((p * groups + q, (q * copies + r) * groups + a))
    return pairs


def to_mirror(values):
    return lax.ppermute(values, ("src", "tgt"), mirror_pairs())


def call(body, name, outs, scalars, arrays, scratch=(), flops=0, limit=12):
    smem = pl.BlockSpec(memory_space=pltpu.SMEM)
    vmem = pl.BlockSpec(memory_space=pltpu.VMEM)
    return pl.pallas_call(
        body,
        in_specs=[smem] * len(scalars) + [vmem] * len(arrays),
        out_specs=[vmem] * len(outs),
        scratch_shapes=list(scratch),
        out_shape=list(outs),
        name=name,
        compiler_params=pltpu.CompilerParams(vmem_limit_bytes=limit * MIB),
        cost_estimate=pl.CostEstimate(flops=flops, bytes_accessed=0, transcendentals=0),
    )(*scalars, *arrays)


def reverse_column(reverse_row):
    return jnp.broadcast_to(reverse_row[...], (8, reverse_row.shape[1])).T[:, :1]


def own_mirror():
    copies = lax.axis_size("src") // lax.axis_size("tgt")
    return lax.axis_index("src") // copies == lax.axis_index("tgt")


def like(shape, dtype):
    return jax.ShapeDtypeStruct(shape, dtype)


def project_body(w_proj_t, state, out, *parts):
    out[...] = dot_nt(w_proj_t[0], state[...]).astype(BF16)
    start = 0
    for part in parts:
        part[...] = state[pl.ds(start, part.shape[0]), :]
        start += part.shape[0]


def project(w_proj_t, state, sizes):
    width, features = w_proj_t.shape[1:]
    return call(
        project_body,
        "project",
        [like((width, state.shape[0]), BF16)] + [like((n, features), BF16) for n in sizes],
        [],
        [w_proj_t, state],
        limit=8,
        flops=PROJECT_FLOPS,
    )


def add_blocks(index, slots, blocks, pool, add):
    mine = lax.axis_index("src")

    def one(slot, carry):
        source = index[slots + slot]
        relative = (source // blocks) ^ mine
        tile = jnp.int32(0)
        place, bit = 1, lax.axis_size("src") // 2
        while place < pool.shape[0]:
            tile = tile + jnp.where((relative & bit) != 0, place, 0)
            place, bit = place * 2, bit // 2
        start = pl.multiple_of((source % blocks) * BLK, BLK)
        into = pl.multiple_of(index[slot] * BLK, BLK)

        @pl.when((relative & 1) == 0)
        def _():
            add(slot, pool[tile, :, pl.ds(start, BLK)], into)

        return carry

    lax.fori_loop(0, jnp.minimum(index[2 * slots], slots), one, 0)


def triplet_body(blocks, own_index, other_index, pool, own_coeffs, other_coeffs, kept, sent, acc):
    acc[...] = jnp.zeros_like(acc)
    for tile, (index, coeffs) in enumerate(
        [(own_index, own_coeffs), (other_index, other_coeffs)]
    ):

        def add(slot, rows, into):
            acc[tile, :, pl.ds(into, BLK)] += dot(rows, coeffs[slot])

        add_blocks(index, coeffs.shape[0], blocks, pool, add)
    kept[...] = acc[0]
    sent[...] = acc[1].astype(BF16)


def triplet_partials(index, pool, coeffs):
    width, edges = pool.shape[1:]
    return call(
        functools.partial(triplet_body, edges // BLK),
        "triplets",
        [like((width, edges), F32), like((width, edges), BF16)],
        index,
        [pool] + coeffs,
        scratch=[pltpu.VMEM((2, width, edges), F32)],
        limit=8,
    )


def branch_of(x, agg, w_up, w_in, w_out, gain):
    summed = x.astype(F32) + dot(agg, w_up[...])
    scale_inv = lax.rsqrt(jnp.mean(summed * summed, axis=-1, keepdims=True) + 1e-06)
    normed = (gain[...] * summed * scale_inv).astype(BF16)
    u = dot(normed, w_in[...])
    activated = (u / (1.0 + jnp.exp(-u))).astype(BF16)
    return summed, dot(activated, w_out[...]).astype(BF16)


def chunks(edges):
    step = min(ROWS, edges)
    return [pl.ds(i, step) for i in range(0, edges, step)]


def weights_of(layer_index, w_up, w_in, w_out, gain):
    return [w.at[layer_index] for w in (w_up, w_in, w_out)] + [gain.at[pl.ds(layer_index, 1)]]


def picking(column, rows, edges):
    lanes = lax.broadcasted_iota(jnp.int32, (rows.size, edges), 1)
    return (column[rows.start : rows.start + rows.size] == lanes).astype(BF16)


def first_body(w_up, w_in, w_out, gain, w_proj_t, agg_t, reverse, *rest):
    weights = weights_of(0, w_up, w_in, w_out, gain)
    agg = agg_t[...].astype(F32).T.astype(BF16)
    w_next = w_proj_t[1]
    *parts, total, branch, v_t, u_t = rest
    state = jnp.concatenate([part[...] for part in parts], axis=0)
    edges = state.shape[0]
    for rows in chunks(edges):
        summed, out = branch_of(state[rows.start : rows.start + rows.size], agg[rows.start : rows.start + rows.size], *weights)
        branch[rows, :] = out
        total[rows, :] = summed + out.astype(F32)
    u = dot_nt(w_next, branch[...]).astype(BF16)
    at = lax.broadcasted_iota(jnp.int32, (edges, edges), 0)
    turned = dot_nt(u, (reverse[...] == at).astype(BF16))
    v = dot_nt(w_next, total[...].astype(BF16))
    u_t[...] = turned.astype(BF16)
    v_t[...] = jnp.where(own_mirror(), v + turned, v).astype(BF16)


def combine_body(v_t, u_mirror, out):
    v = v_t[...].astype(F32)
    out[0] = jnp.where(own_mirror(), v, v + u_mirror[...].astype(F32)).astype(BF16)


def combine_pair_body(v_t, v_other, u_mirror, u_across, out):
    v, other = v_t[...].astype(F32), v_other[...].astype(F32)
    here = own_mirror()
    out[0] = jnp.where(here, v, v + u_mirror[...].astype(F32)).astype(BF16)
    out[1] = jnp.where(here, other + u_across[...].astype(F32), other).astype(BF16)


def second_body(
    w_up, w_in, w_out, gain, agg_t, agg_other, reverse, total, branch, *rest
):
    edges = total.shape[0]
    weights = weights_of(0, w_up, w_in, w_out, gain)
    here = own_mirror()
    *parts, state, mirrored = rest
    own, other = parts[: len(parts) // 2], parts[len(parts) // 2 :]
    source = jnp.concatenate(
        [jnp.where(here, x[...], y[...]) for x, y in zip(own, other)], axis=0
    )
    low = jnp.where(here, agg_t[...], agg_other[...])
    column = reverse_column(reverse)
    for rows in chunks(edges):
        pick = picking(column, rows, edges)
        summed, out = branch_of(dot(pick, source), dot_nt(pick, low).astype(BF16), *weights)
        state[rows, :] = (total[rows, :] + out.astype(F32)).astype(BF16)
        mirrored[rows, :] = (summed + out.astype(F32) + branch[rows, :].astype(F32)).astype(BF16)


def third_body(w_up, w_in, w_out, gain, state, agg_t, total):
    weights = weights_of(1, w_up, w_in, w_out, gain)
    agg = agg_t[...].astype(F32).T.astype(BF16)
    for rows in chunks(state.shape[0]):
        summed, out = branch_of(state[rows, :], agg[rows.start : rows.start + rows.size], *weights)
        total[rows, :] = summed + out.astype(F32)


def last_body(w_up, w_in, w_out, gain, mirrored, agg_t, agg_other, reverse, total, state):
    edges = total.shape[0]
    weights = weights_of(1, w_up, w_in, w_out, gain)
    low = jnp.where(own_mirror(), agg_t[...], agg_other[...])
    at = lax.broadcasted_iota(jnp.int32, (edges, edges), 0)
    agg = dot(low, (reverse[...] == at).astype(BF16)).T.astype(BF16)
    for rows in chunks(edges):
        summed, out = branch_of(
            mirrored[rows, :], agg[rows.start : rows.start + rows.size], *weights
        )
        state[rows, :] = (total[rows, :] + out.astype(F32)).astype(BF16)


def gather_step(held, bit):
    return jnp.concatenate([held, hop(held, bit)], axis=0)


def part_sizes(edges):
    half = edges // 2
    cut = max(16, half * EARLY // 16 // 16 * 16)
    return [cut, half - cut, cut, half - cut]


def second_route_x(values):
    groups, size = lax.axis_size("tgt"), lax.axis_size("src")
    if groups != 2:
        return values
    copies = size // groups
    pairs = [
        ((a * copies + r) * 2 + 1 - a, (a * copies + r) * 2 + a)
        for a in range(2)
        for r in range(copies)
    ]
    return lax.ppermute(values, ("src", "tgt"), pairs)


def second_route_z(turned, values):
    groups, size = lax.axis_size("tgt"), lax.axis_size("src")
    if groups != 2:
        return to_mirror(values)
    copies = size // groups
    pairs = [
        ((a * copies + r) * 2 + a, ((1 - a) * copies + r) * 2 + a)
        for a in range(2)
        for r in range(copies)
    ]
    return lax.ppermute(turned, ("src", "tgt"), pairs)


def gather_down(held, last):
    bit = lax.axis_size("src") // 2 // held.shape[0]
    while bit >= last:
        held = gather_step(held, bit)
        bit //= 2
    return held


def next_pool(v_t, u_t):
    size, groups = lax.axis_size("src"), lax.axis_size("tgt")
    u_mirror = to_mirror(u_t)
    if groups != 2:
        held = call(combine_body, "combine", [like((1,) + v_t.shape, BF16)], [], [v_t, u_mirror])[0]
        return gather_down(held, 4)
    v_other = hop(v_t, size // 2)
    copies = size // 2
    pairs = [
        ((a * copies + r) * 2 + 1 - a, (a * copies + r) * 2 + a)
        for a in range(2)
        for r in range(copies)
    ]
    u_across = lax.ppermute(u_t, ("src", "tgt"), pairs)
    held = call(
        combine_pair_body,
        "combine",
        [like((2,) + v_t.shape, BF16)],
        [],
        [v_t, v_other, u_mirror, u_across],
        limit=4,
    )[0]
    return gather_down(held, 4)


def sum_over_cores(kept, sent):
    return (kept + hop(sent, 1).astype(F32)).astype(BF16)


def local(
    edge_states,
    triplet_coeff,
    block_target,
    block_source,
    block_count,
    reverse_slot,
    w_proj,
    w_up,
    w_in,
    w_out,
    norm_gain,
):
    state0 = edge_states[0, 0]
    edges, features = state0.shape
    width = w_proj.shape[2]
    reverse = reverse_slot[0]
    w_proj_t = jnp.swapaxes(w_proj, 1, 2)
    weights = [w_up, w_in, w_out, norm_gain]

    own_index = jnp.concatenate([block_target[0, 0], block_source[0, 0], block_count[0]])
    own_coeffs = triplet_coeff[0, 0]
    index, coeffs = [own_index, hop(own_index, 1)], [own_coeffs, hop(own_coeffs, 1)]
    proj0, *parts = project(w_proj_t, state0, part_sizes(edges))
    turned = [second_route_x(part) for part in parts[2:]]
    pool = gather_down(proj0[None], 4)
    index, coeffs, direct, turned[0], pool = lax.optimization_barrier(
        (index, coeffs, parts[0], turned[0], pool)
    )
    early = [to_mirror(direct), second_route_z(turned[0], parts[2])]
    agg0 = sum_over_cores(*triplet_partials(index, gather_down(pool, 2), coeffs))
    total0, branch0, v_t, u_t = call(
        first_body,
        "first",
        [
            like((edges, features), F32),
            like((edges, features), BF16),
            like((width, edges), BF16),
            like((width, edges), BF16),
        ],
        [],
        weights + [w_proj_t, agg0, reverse] + parts,
    )
    u_t, v_t, early, turned[1] = lax.optimization_barrier((u_t, v_t, early, turned[1]))
    pool1 = next_pool(v_t, u_t)
    direct, turned[1], agg0_held, pool1 = lax.optimization_barrier(
        (parts[1], turned[1], agg0, pool1)
    )
    agg0_other = to_mirror(agg0_held)
    late = [to_mirror(direct), second_route_z(turned[1], parts[3])]
    kept, sent = triplet_partials(index, gather_down(pool1, 2), coeffs)
    agg0_other, late, sent = lax.optimization_barrier((agg0_other, late, sent))
    agg1 = sum_over_cores(kept, sent)
    agg1_other = to_mirror(agg1)
    state1, mirrored1 = call(
        second_body,
        "second",
        [like((edges, features), BF16), like((edges, features), BF16)],
        [],
        weights
        + [agg0, agg0_other, reverse, total0, branch0]
        + parts
        + [early[0], late[0], early[1], late[1]],
    )
    total1 = call(
        third_body,
        "third",
        [like((edges, features), F32)],
        [],
        weights + [state1, agg1],
    )[0]
    final = call(
        last_body,
        "last",
        [like((edges, features), BF16)],
        [],
        weights + [mirrored1, agg1, agg1_other, reverse, total1],
    )[0]
    return final[None, None]


def solution(mesh):
    return jax.shard_map(
        local,
        mesh=mesh,
        in_specs=(
            P("src", "tgt", None, None),
            P("src", "tgt", None, None, None),
            P("src", "tgt", None),
            P("src", "tgt", None),
            P("src", "tgt"),
            P("src", "tgt", None),
            P(),
            P(),
            P(),
            P(),
            P(),
        ),
        out_specs=P("src", "tgt", None, None),
        check_vma=False,
    )
```

```python
import functools

import jax
import jax.numpy as jnp
from jax import lax
from jax.experimental import pallas as pl
from jax.experimental.pallas import tpu as pltpu
from jax.sharding import PartitionSpec as P

BLK = 128
LAYERS = 2
ROWS = 512
LATE = 4
PROJECT_FLOPS = 10 * 1153 * 10**6
MIB = 2**20
F32 = jnp.float32
BF16 = jnp.bfloat16


def dot(x, y):
    return jnp.dot(x, y, preferred_element_type=F32)


def dot_nt(x, y):
    return lax.dot_general(x, y, (((1,), (1,)), ((), ())), preferred_element_type=F32)


def hop(values, bit):
    size = lax.axis_size("src")
    return lax.ppermute(values, "src", [(i, i ^ bit) for i in range(size)])


def mirror_pairs():
    groups = lax.axis_size("tgt")
    copies = lax.axis_size("src") // groups
    pairs = []
    for p in range(groups * copies):
        a, r = divmod(p, copies)
        for q in range(groups):
            if a != q:
                pairs.append((p * groups + q, (q * copies + r) * groups + a))
    return pairs


def to_mirror(values):
    return lax.ppermute(values, ("src", "tgt"), mirror_pairs())


def call(body, name, outs, scalars, arrays, scratch=(), flops=0, limit=12):
    smem = pl.BlockSpec(memory_space=pltpu.SMEM)
    vmem = pl.BlockSpec(memory_space=pltpu.VMEM)
    return pl.pallas_call(
        body,
        in_specs=[smem] * len(scalars) + [vmem] * len(arrays),
        out_specs=[vmem] * len(outs),
        scratch_shapes=list(scratch),
        out_shape=list(outs),
        name=name,
        compiler_params=pltpu.CompilerParams(vmem_limit_bytes=limit * MIB),
        cost_estimate=pl.CostEstimate(flops=flops, bytes_accessed=0, transcendentals=0),
    )(*scalars, *arrays)


def reverse_column(reverse_row):
    return jnp.broadcast_to(reverse_row[...], (8, reverse_row.shape[1])).T[:, :1]


def own_mirror():
    copies = lax.axis_size("src") // lax.axis_size("tgt")
    return lax.axis_index("src") // copies == lax.axis_index("tgt")


def like(shape, dtype):
    return jax.ShapeDtypeStruct(shape, dtype)


def project_body(w_proj_t, state, out, *parts):
    out[...] = dot_nt(w_proj_t[0], state[...]).astype(BF16)
    start = 0
    for part in parts:
        part[...] = state[pl.ds(start, part.shape[0]), :]
        start += part.shape[0]


def project(w_proj_t, state, sizes):
    width, features = w_proj_t.shape[1:]
    return call(
        project_body,
        "project",
        [like((width, state.shape[0]), BF16)] + [like((n, features), BF16) for n in sizes],
        [],
        [w_proj_t, state],
        limit=8,
        flops=PROJECT_FLOPS,
    )


def add_blocks(index, slots, blocks, pool, add):
    mine = lax.axis_index("src")

    def one(slot, carry):
        source = index[slots + slot]
        relative = (source // blocks) ^ mine
        tile = jnp.int32(0)
        place, bit = 1, lax.axis_size("src") // 2
        while place < pool.shape[0]:
            tile = tile + jnp.where((relative & bit) != 0, place, 0)
            place, bit = place * 2, bit // 2
        start = pl.multiple_of((source % blocks) * BLK, BLK)
        into = pl.multiple_of(index[slot] * BLK, BLK)

        @pl.when((relative & 1) == 0)
        def _():
            add(slot, pool[tile, :, pl.ds(start, BLK)], into)

        return carry

    lax.fori_loop(0, jnp.minimum(index[2 * slots], slots), one, 0)


def triplet_body(blocks, own_index, other_index, pool, own_coeffs, other_coeffs, kept, sent, acc):
    acc[...] = jnp.zeros_like(acc)
    for tile, (index, coeffs) in enumerate(
        [(own_index, own_coeffs), (other_index, other_coeffs)]
    ):

        def add(slot, rows, into):
            acc[tile, :, pl.ds(into, BLK)] += dot(rows, coeffs[slot])

        add_blocks(index, coeffs.shape[0], blocks, pool, add)
    kept[...] = acc[0]
    sent[...] = acc[1].astype(BF16)


def triplet_partials(index, pool, coeffs):
    width, edges = pool.shape[1:]
    return call(
        functools.partial(triplet_body, edges // BLK),
        "triplets",
        [like((width, edges), F32), like((width, edges), BF16)],
        index,
        [pool] + coeffs,
        scratch=[pltpu.VMEM((2, width, edges), F32)],
        limit=8,
    )


def branch_of(x, agg, w_up, w_in, w_out, gain):
    summed = x.astype(F32) + dot(agg, w_up[...])
    scale_inv = lax.rsqrt(jnp.mean(summed * summed, axis=-1, keepdims=True) + 1e-06)
    normed = (gain[...] * summed * scale_inv).astype(BF16)
    u = dot(normed, w_in[...])
    activated = (u / (1.0 + jnp.exp(-u))).astype(BF16)
    return summed, dot(activated, w_out[...]).astype(BF16)


def chunks(edges):
    step = min(ROWS, edges)
    return [pl.ds(i, step) for i in range(0, edges, step)]


def weights_of(layer_index, w_up, w_in, w_out, gain):
    return [w.at[layer_index] for w in (w_up, w_in, w_out)] + [gain.at[pl.ds(layer_index, 1)]]


def picking(column, rows, edges):
    lanes = lax.broadcasted_iota(jnp.int32, (rows.size, edges), 1)
    return (column[rows.start : rows.start + rows.size] == lanes).astype(BF16)


def first_body(w_up, w_in, w_out, gain, w_proj_t, agg_t, reverse, *rest):
    weights = weights_of(0, w_up, w_in, w_out, gain)
    agg = agg_t[...].astype(F32).T.astype(BF16)
    w_next = w_proj_t[1]
    *parts, total, branch, v_t, u_t, late = rest
    state = jnp.concatenate([part[...] for part in parts], axis=0)
    edges = state.shape[0]
    for rows in chunks(edges):
        summed, out = branch_of(state[rows.start : rows.start + rows.size], agg[rows.start : rows.start + rows.size], *weights)
        branch[rows, :] = out
        total[rows, :] = summed + out.astype(F32)
    u = dot_nt(w_next, branch[...]).astype(BF16)
    at = lax.broadcasted_iota(jnp.int32, (edges, edges), 0)
    turned = dot_nt(u, (reverse[...] == at).astype(BF16))
    v = dot_nt(w_next, total[...].astype(BF16))
    u_t[...] = turned.astype(BF16)
    v_t[...] = jnp.where(own_mirror(), v + turned, v).astype(BF16)
    rows, low = parts[1].shape[0], agg_t.shape[0] * edges // state.shape[1]
    late[:rows, :] = parts[1][...]
    for k in range(agg_t.shape[0] // low):
        late[rows:, pl.ds(k * edges, edges)] = agg_t[pl.ds(k * low, low), :]


def combine_body(v_t, u_mirror, out):
    v = v_t[...].astype(F32)
    out[0] = jnp.where(own_mirror(), v, v + u_mirror[...].astype(F32)).astype(BF16)


def combine_pair_body(v_t, v_other, u_mirror, u_across, out):
    v, other = v_t[...].astype(F32), v_other[...].astype(F32)
    here = own_mirror()
    out[0] = jnp.where(here, v, v + u_mirror[...].astype(F32)).astype(BF16)
    out[1] = jnp.where(here, other + u_across[...].astype(F32), other).astype(BF16)


def second_body(w_up, w_in, w_out, gain, agg_t, reverse, total, branch, *rest):
    edges = total.shape[0]
    weights = weights_of(0, w_up, w_in, w_out, gain)
    here = own_mirror()
    *parts, state, mirrored = rest
    own, other = parts[:3], parts[3:]
    rows = own[1].shape[0]
    source = jnp.where(
        here,
        jnp.concatenate([x[...] for x in own], axis=0),
        jnp.concatenate([other[0][...], other[1][:rows, :], other[2][...], other[3][...]], axis=0),
    )
    fold = own[1].shape[1] // edges
    agg_other = jnp.concatenate(
        [other[1][rows:, pl.ds(k * edges, edges)] for k in range(fold)], axis=0
    )
    low = jnp.where(here, agg_t[...], agg_other)
    column = reverse_column(reverse)
    for rows in chunks(edges):
        pick = picking(column, rows, edges)
        summed, out = branch_of(dot(pick, source), dot_nt(pick, low).astype(BF16), *weights)
        state[rows, :] = (total[rows, :] + out.astype(F32)).astype(BF16)
        mirrored[rows, :] = (summed + out.astype(F32) + branch[rows, :].astype(F32)).astype(BF16)


def third_body(w_up, w_in, w_out, gain, state, agg_t, total):
    weights = weights_of(1, w_up, w_in, w_out, gain)
    agg = agg_t[...].astype(F32).T.astype(BF16)
    for rows in chunks(state.shape[0]):
        summed, out = branch_of(state[rows, :], agg[rows.start : rows.start + rows.size], *weights)
        total[rows, :] = summed + out.astype(F32)


def last_body(w_up, w_in, w_out, gain, mirrored, agg_t, agg_other, reverse, total, state):
    edges = total.shape[0]
    weights = weights_of(1, w_up, w_in, w_out, gain)
    low = jnp.where(own_mirror(), agg_t[...], agg_other[...])
    at = lax.broadcasted_iota(jnp.int32, (edges, edges), 0)
    agg = dot(low, (reverse[...] == at).astype(BF16)).T.astype(BF16)
    for rows in chunks(edges):
        summed, out = branch_of(
            mirrored[rows, :], agg[rows.start : rows.start + rows.size], *weights
        )
        state[rows, :] = (total[rows, :] + out.astype(F32)).astype(BF16)


def gather_step(held, bit):
    return jnp.concatenate([held, hop(held, bit)], axis=0)


def part_sizes(edges):
    unit = max(16, edges // 32)
    late = LATE * unit
    direct = (edges - 2 * late) // 2 - unit
    return [direct, late, edges - late - direct]


def second_route_x(values):
    groups, size = lax.axis_size("tgt"), lax.axis_size("src")
    if groups != 2:
        return values
    copies = size // groups
    pairs = [
        ((a * copies + r) * 2 + 1 - a, (a * copies + r) * 2 + a)
        for a in range(2)
        for r in range(copies)
    ]
    return lax.ppermute(values, ("src", "tgt"), pairs)


def second_route_z(turned, values):
    groups, size = lax.axis_size("tgt"), lax.axis_size("src")
    if groups != 2:
        return to_mirror(values)
    copies = size // groups
    pairs = [
        ((a * copies + r) * 2 + a, ((1 - a) * copies + r) * 2 + a)
        for a in range(2)
        for r in range(copies)
    ]
    return lax.ppermute(turned, ("src", "tgt"), pairs)


def gather_down(held, last):
    bit = lax.axis_size("src") // 2 // held.shape[0]
    while bit >= last:
        held = gather_step(held, bit)
        bit //= 2
    return held


def next_pool(v_t, u_t):
    size, groups = lax.axis_size("src"), lax.axis_size("tgt")
    u_mirror = to_mirror(u_t)
    if groups != 2:
        held = call(combine_body, "combine", [like((1,) + v_t.shape, BF16)], [], [v_t, u_mirror])[0]
        return gather_down(held, 4)
    v_other = hop(v_t, size // 2)
    copies = size // 2
    pairs = [
        ((a * copies + r) * 2 + 1 - a, (a * copies + r) * 2 + a)
        for a in range(2)
        for r in range(copies)
    ]
    u_across = lax.ppermute(u_t, ("src", "tgt"), pairs)
    held = call(
        combine_pair_body,
        "combine",
        [like((2,) + v_t.shape, BF16)],
        [],
        [v_t, v_other, u_mirror, u_across],
        limit=4,
    )[0]
    return gather_down(held, 4)


def sum_over_cores(kept, sent):
    return (kept + hop(sent, 1).astype(F32)).astype(BF16)


def local(
    edge_states,
    triplet_coeff,
    block_target,
    block_source,
    block_count,
    reverse_slot,
    w_proj,
    w_up,
    w_in,
    w_out,
    norm_gain,
):
    state0 = edge_states[0, 0]
    edges, features = state0.shape
    width = w_proj.shape[2]
    reverse = reverse_slot[0]
    w_proj_t = jnp.swapaxes(w_proj, 1, 2)
    weights = [w_up, w_in, w_out, norm_gain]

    own_index = jnp.concatenate([block_target[0, 0], block_source[0, 0], block_count[0]])
    own_coeffs = triplet_coeff[0, 0]
    index, coeffs = [own_index, hop(own_index, 1)], [own_coeffs, hop(own_coeffs, 1)]
    proj0, *parts = project(w_proj_t, state0, part_sizes(edges))
    turned = second_route_x(parts[2])
    pool = gather_down(proj0[None], 4)
    index, coeffs, direct, turned, pool = lax.optimization_barrier(
        (index, coeffs, parts[0], turned, pool)
    )
    cut = parts[2].shape[0] - parts[1].shape[0]
    early = [to_mirror(direct), second_route_z(turned[:cut], parts[2][:cut])]
    agg0 = sum_over_cores(*triplet_partials(index, gather_down(pool, 2), coeffs))
    total0, branch0, v_t, u_t, late_direct = call(
        first_body,
        "first",
        [
            like((edges, features), F32),
            like((edges, features), BF16),
            like((width, edges), BF16),
            like((width, edges), BF16),
            like((parts[1].shape[0] + width * edges // features, features), BF16),
        ],
        [],
        weights + [w_proj_t, agg0, reverse] + parts,
    )
    u_t, v_t, early = lax.optimization_barrier((u_t, v_t, early))
    pool1 = next_pool(v_t, u_t)
    late_direct, turned, pool1 = lax.optimization_barrier((late_direct, turned, pool1))
    late = [to_mirror(late_direct), second_route_z(turned[cut:], parts[2][cut:])]
    kept, sent = triplet_partials(index, gather_down(pool1, 2), coeffs)
    late, sent = lax.optimization_barrier((late, sent))
    agg1 = sum_over_cores(kept, sent)
    state1, mirrored1 = call(
        second_body,
        "second",
        [like((edges, features), BF16), like((edges, features), BF16)],
        [],
        weights
        + [agg0, reverse, total0, branch0]
        + parts
        + [early[0], late[0], early[1], late[1]],
    )
    agg1, state1, mirrored1 = lax.optimization_barrier((agg1, state1, mirrored1))
    agg1_other = to_mirror(agg1)
    total1 = call(
        third_body,
        "third",
        [like((edges, features), F32)],
        [],
        weights + [state1, agg1],
    )[0]
    final = call(
        last_body,
        "last",
        [like((edges, features), BF16)],
        [],
        weights + [mirrored1, agg1, agg1_other, reverse, total1],
    )[0]
    return final[None, None]


def solution(mesh):
    return jax.shard_map(
        local,
        mesh=mesh,
        in_specs=(
            P("src", "tgt", None, None),
            P("src", "tgt", None, None, None),
            P("src", "tgt", None),
            P("src", "tgt", None),
            P("src", "tgt"),
            P("src", "tgt", None),
            P(),
            P(),
            P(),
            P(),
            P(),
        ),
        out_specs=P("src", "tgt", None, None),
        check_vma=False,
    )
```

```python
import functools

import jax
import jax.numpy as jnp
from jax import lax
from jax.experimental import pallas as pl
from jax.experimental.pallas import tpu as pltpu
from jax.sharding import PartitionSpec as P

BLK = 128
LAYERS = 2
ROWS = 512
PARTS = (4, 4)
PROJECT_FLOPS = 10 * 1153 * 10**6
SECOND_FLOPS = 5 * 1153 * 10**6
MIB = 2**20
F32 = jnp.float32
BF16 = jnp.bfloat16


def dot(x, y):
    return jnp.dot(x, y, preferred_element_type=F32)


def dot_nt(x, y):
    return lax.dot_general(x, y, (((1,), (1,)), ((), ())), preferred_element_type=F32)


def hop(values, bit):
    size = lax.axis_size("src")
    return lax.ppermute(values, "src", [(i, i ^ bit) for i in range(size)])


def mirror_pairs():
    groups = lax.axis_size("tgt")
    copies = lax.axis_size("src") // groups
    pairs = []
    for p in range(groups * copies):
        a, r = divmod(p, copies)
        for q in range(groups):
            if a != q:
                pairs.append((p * groups + q, (q * copies + r) * groups + a))
    return pairs


def to_mirror(values):
    return lax.ppermute(values, ("src", "tgt"), mirror_pairs())


def call(body, name, outs, scalars, arrays, scratch=(), flops=0, limit=12):
    smem = pl.BlockSpec(memory_space=pltpu.SMEM)
    vmem = pl.BlockSpec(memory_space=pltpu.VMEM)
    return pl.pallas_call(
        body,
        in_specs=[smem] * len(scalars) + [vmem] * len(arrays),
        out_specs=[vmem] * len(outs),
        scratch_shapes=list(scratch),
        out_shape=list(outs),
        name=name,
        compiler_params=pltpu.CompilerParams(vmem_limit_bytes=limit * MIB),
        cost_estimate=pl.CostEstimate(flops=flops, bytes_accessed=0, transcendentals=0),
    )(*scalars, *arrays)


def reverse_column(reverse_row):
    return jnp.broadcast_to(reverse_row[...], (8, reverse_row.shape[1])).T[:, :1]


def own_mirror():
    copies = lax.axis_size("src") // lax.axis_size("tgt")
    return lax.axis_index("src") // copies == lax.axis_index("tgt")


def like(shape, dtype):
    return jax.ShapeDtypeStruct(shape, dtype)


def by_core(on_first, on_second):
    return jnp.where(lax.axis_index("src") % 2 == 0, on_first, on_second)


def project_body(w_proj_t, state, out, *parts):
    out[...] = dot_nt(w_proj_t[0], state[...]).astype(BF16)
    half, start, count = state.shape[0] // 2, 0, len(parts) // 2
    for keep, swap in zip(parts[:count], parts[count:]):
        rows = keep.shape[0]
        low, high = state[pl.ds(start, rows), :], state[pl.ds(half + start, rows), :]
        keep[...] = by_core(low, high)
        swap[...] = by_core(high, low)
        start += rows


def project(w_proj_t, state):
    width, (edges, features) = w_proj_t.shape[1], state.shape
    sizes = [edges // 2 * part // sum(PARTS) for part in PARTS]
    outs = call(
        project_body,
        "project",
        [like((width, edges), BF16)] + [like((n, features), BF16) for n in sizes * 2],
        [],
        [w_proj_t, state],
        limit=8,
        flops=PROJECT_FLOPS,
    )
    return outs[0], outs[1 : 1 + len(sizes)], outs[1 + len(sizes) :]


def add_blocks(index, slots, blocks, pool, add):
    mine = lax.axis_index("src")

    def one(slot, carry):
        source = index[slots + slot]
        relative = (source // blocks) ^ mine
        tile = jnp.int32(0)
        place, bit = 1, lax.axis_size("src") // 2
        while place < pool.shape[0]:
            tile = tile + jnp.where((relative & bit) != 0, place, 0)
            place, bit = place * 2, bit // 2
        start = pl.multiple_of((source % blocks) * BLK, BLK)
        into = pl.multiple_of(index[slot] * BLK, BLK)

        @pl.when((relative & 1) == 0)
        def _():
            add(slot, pool[tile, :, pl.ds(start, BLK)], into)

        return carry

    lax.fori_loop(0, jnp.minimum(index[2 * slots], slots), one, 0)


def triplet_body(blocks, own_index, other_index, pool, own_coeffs, other_coeffs, kept, sent, acc):
    acc[...] = jnp.zeros_like(acc)
    for tile, (index, coeffs) in enumerate(
        [(own_index, own_coeffs), (other_index, other_coeffs)]
    ):

        def add(slot, rows, into):
            acc[tile, :, pl.ds(into, BLK)] += dot(rows, coeffs[slot])

        add_blocks(index, coeffs.shape[0], blocks, pool, add)
    kept[...] = acc[0]
    sent[...] = acc[1].astype(BF16)


def triplet_partials(index, pool, coeffs):
    width, edges = pool.shape[1:]
    return call(
        functools.partial(triplet_body, edges // BLK),
        "triplets",
        [like((width, edges), F32), like((width, edges), BF16)],
        index,
        [pool] + coeffs,
        scratch=[pltpu.VMEM((2, width, edges), F32)],
        limit=8,
    )


def branch_of(x, agg, w_up, w_in, w_out, gain):
    summed = x.astype(F32) + dot(agg, w_up[...])
    scale_inv = lax.rsqrt(jnp.mean(summed * summed, axis=-1, keepdims=True) + 1e-06)
    normed = (gain[...] * summed * scale_inv).astype(BF16)
    u = dot(normed, w_in[...])
    activated = (u / (1.0 + jnp.exp(-u))).astype(BF16)
    return summed, dot(activated, w_out[...]).astype(BF16)


def chunks(edges):
    step = min(ROWS, edges)
    return [pl.ds(i, step) for i in range(0, edges, step)]


def weights_of(layer_index, w_up, w_in, w_out, gain):
    return [w.at[layer_index] for w in (w_up, w_in, w_out)] + [gain.at[pl.ds(layer_index, 1)]]


def picking(column, rows, edges):
    lanes = lax.broadcasted_iota(jnp.int32, (rows.size, edges), 1)
    return (column[rows.start : rows.start + rows.size] == lanes).astype(BF16)


def first_body(
    w_up, w_in, w_out, gain, w_proj_t, agg_t, reverse, state, total, branch, v_t, u_t
):
    weights = weights_of(0, w_up, w_in, w_out, gain)
    agg = agg_t[...].astype(F32).T.astype(BF16)
    w_next = w_proj_t[1]
    edges = state.shape[0]
    for rows in chunks(edges):
        summed, out = branch_of(state[rows, :], agg[rows.start : rows.start + rows.size], *weights)
        branch[rows, :] = out
        total[rows, :] = summed + out.astype(F32)
    u = dot_nt(w_next, branch[...]).astype(BF16)
    at = lax.broadcasted_iota(jnp.int32, (edges, edges), 0)
    turned = dot_nt(u, (reverse[...] == at).astype(BF16))
    v = dot_nt(w_next, total[...].astype(BF16))
    u_t[...] = turned.astype(BF16)
    v_t[...] = jnp.where(own_mirror(), v + turned, v).astype(BF16)


def combine_body(v_t, u_mirror, out):
    v = v_t[...].astype(F32)
    out[0] = jnp.where(own_mirror(), v, v + u_mirror[...].astype(F32)).astype(BF16)


def combine_pair_body(v_t, v_other, u_mirror, u_across, out):
    v, other = v_t[...].astype(F32), v_other[...].astype(F32)
    here = own_mirror()
    out[0] = jnp.where(here, v, v + u_mirror[...].astype(F32)).astype(BF16)
    out[1] = jnp.where(here, other + u_across[...].astype(F32), other).astype(BF16)


def second_body(
    w_up, w_in, w_out, gain, agg_t, agg_other, reverse, total, branch, own, *rest
):
    edges = total.shape[0]
    weights = weights_of(0, w_up, w_in, w_out, gain)
    here = own_mirror()
    *other, state, mirrored = rest
    if len(other) == 1:
        received = other[0][...]
    else:
        count = len(other) // 2
        passed = jnp.concatenate([y[...] for y in other[count:]], axis=0)
        routed = jnp.concatenate([x[: y.shape[0], :] for x, y in zip(other, other[count:])], axis=0)
        received = jnp.concatenate([by_core(routed, passed), by_core(passed, routed)], axis=0)
    source = jnp.where(here, own[...], received)
    low = jnp.where(here, agg_t[...], agg_other[...])
    column = reverse_column(reverse)
    for rows in chunks(edges):
        pick = picking(column, rows, edges)
        summed, out = branch_of(dot(pick, source), dot_nt(pick, low).astype(BF16), *weights)
        state[rows, :] = (total[rows, :] + out.astype(F32)).astype(BF16)
        mirrored[rows, :] = (summed + out.astype(F32) + branch[rows, :].astype(F32)).astype(BF16)


def third_body(w_up, w_in, w_out, gain, state, agg_t, total):
    weights = weights_of(1, w_up, w_in, w_out, gain)
    agg = agg_t[...].astype(F32).T.astype(BF16)
    for rows in chunks(state.shape[0]):
        summed, out = branch_of(state[rows, :], agg[rows.start : rows.start + rows.size], *weights)
        total[rows, :] = summed + out.astype(F32)


def last_body(w_up, w_in, w_out, gain, mirrored, agg_t, agg_other, reverse, total, state):
    edges = total.shape[0]
    weights = weights_of(1, w_up, w_in, w_out, gain)
    low = jnp.where(own_mirror(), agg_t[...], agg_other[...])
    at = lax.broadcasted_iota(jnp.int32, (edges, edges), 0)
    agg = dot(low, (reverse[...] == at).astype(BF16)).T.astype(BF16)
    for rows in chunks(edges):
        summed, out = branch_of(
            mirrored[rows, :], agg[rows.start : rows.start + rows.size], *weights
        )
        state[rows, :] = (total[rows, :] + out.astype(F32)).astype(BF16)


def gather_step(held, bit):
    return jnp.concatenate([held, hop(held, bit)], axis=0)


def stage_routes(keep, swap):
    message = jnp.concatenate([keep, hop(swap, 1)], axis=0)
    copies = lax.axis_size("src") // 2
    pairs = []
    for a in range(2):
        for r in range(copies):
            row = (a * copies + r) * 2
            pairs += [(row + 1 - a, row + a)] if r % 2 else [(row, row), (row + 1, row + 1)]
    return lax.ppermute(message, ("src", "tgt"), pairs)


def send_routes(staged):
    copies = lax.axis_size("src") // 2
    pairs = []
    for a in range(2):
        for r in range(copies):
            across = (1 - a) * copies + r
            if r % 2:
                pairs.append(((a * copies + r) * 2 + a, across * 2 + a))
            else:
                pairs.append(((a * copies + r) * 2 + 1 - a, across * 2 + a))
    return lax.ppermute(staged, ("src", "tgt"), pairs)


def pass_on(routed):
    return hop(routed[routed.shape[0] // 2 :], 1)


def gather_down(held, last):
    bit = lax.axis_size("src") // 2 // held.shape[0]
    while bit >= last:
        held = gather_step(held, bit)
        bit //= 2
    return held


def next_pool(v_t, u_t):
    size, groups = lax.axis_size("src"), lax.axis_size("tgt")
    u_mirror = to_mirror(u_t)
    if groups != 2:
        return call(combine_body, "combine", [like((1,) + v_t.shape, BF16)], [], [v_t, u_mirror])[0]
    v_other = hop(v_t, size // 2)
    copies = size // 2
    pairs = [
        ((a * copies + r) * 2 + 1 - a, (a * copies + r) * 2 + a)
        for a in range(2)
        for r in range(copies)
    ]
    u_across = lax.ppermute(u_t, ("src", "tgt"), pairs)
    return call(
        combine_pair_body,
        "combine",
        [like((2,) + v_t.shape, BF16)],
        [],
        [v_t, v_other, u_mirror, u_across],
        limit=4,
    )[0]


def sum_over_cores(kept, sent):
    return (kept + hop(sent, 1).astype(F32)).astype(BF16)


def local(
    edge_states,
    triplet_coeff,
    block_target,
    block_source,
    block_count,
    reverse_slot,
    w_proj,
    w_up,
    w_in,
    w_out,
    norm_gain,
):
    state0 = edge_states[0, 0]
    edges, features = state0.shape
    width = w_proj.shape[2]
    reverse = reverse_slot[0]
    w_proj_t = jnp.swapaxes(w_proj, 1, 2)
    weights = [w_up, w_in, w_out, norm_gain]

    own_index = jnp.concatenate([block_target[0, 0], block_source[0, 0], block_count[0]])
    own_coeffs = triplet_coeff[0, 0]
    index, coeffs = [own_index, hop(own_index, 1)], [own_coeffs, hop(own_coeffs, 1)]
    paired = lax.axis_size("tgt") == 2
    paired = lax.axis_size("tgt") == 2
    proj0, keep, swap = project(w_proj_t, state0)
    if paired:
        staged = [stage_routes(x, y) for x, y in zip(keep, swap)]
    else:
        staged = [state0]
    pool = gather_down(proj0[None], 4)
    index, coeffs, pool = lax.optimization_barrier((index, coeffs, pool))
    routed = [send_routes(x) if paired else to_mirror(x) for x in staged]
    agg0 = sum_over_cores(*triplet_partials(index, gather_down(pool, 2), coeffs))
    total0, branch0, v_t, u_t = call(
        first_body,
        "first",
        [
            like((edges, features), F32),
            like((edges, features), BF16),
            like((width, edges), BF16),
            like((width, edges), BF16),
        ],
        [],
        weights + [w_proj_t, agg0, reverse, state0],
    )
    passed = [pass_on(routed[0])] if paired else []
    u_t, v_t, routed, passed = lax.optimization_barrier((u_t, v_t, routed, passed))
    held1 = next_pool(v_t, u_t)
    routed, agg0_sent, held1 = lax.optimization_barrier((routed, agg0, held1))
    received = routed + passed + [pass_on(x) for x in routed[1:] if paired]
    agg0_other = to_mirror(agg0_sent)
    pool1 = gather_down(held1, 4)
    near1 = gather_down(pool1, 2)
    state1, mirrored1 = call(
        second_body,
        "second",
        [like((edges, features), BF16), like((edges, features), BF16)],
        [],
        weights
        + [agg0, agg0_other, reverse, total0, branch0, state0]
        + received,
        flops=SECOND_FLOPS,
    )
    near1, state1, mirrored1 = lax.optimization_barrier((near1, state1, mirrored1))
    kept, sent = triplet_partials(index, near1, coeffs)
    agg1 = sum_over_cores(kept, sent)
    agg1_other = to_mirror(agg1)
    total1 = call(
        third_body,
        "third",
        [like((edges, features), F32)],
        [],
        weights + [state1, agg1],
    )[0]
    final = call(
        last_body,
        "last",
        [like((edges, features), BF16)],
        [],
        weights + [mirrored1, agg1, agg1_other, reverse, total1],
    )[0]
    return final[None, None]


def solution(mesh):
    return jax.shard_map(
        local,
        mesh=mesh,
        in_specs=(
            P("src", "tgt", None, None),
            P("src", "tgt", None, None, None),
            P("src", "tgt", None),
            P("src", "tgt", None),
            P("src", "tgt"),
            P("src", "tgt", None),
            P(),
            P(),
            P(),
            P(),
            P(),
        ),
        out_specs=P("src", "tgt", None, None),
        check_vma=False,
    )
```

```python
import functools

import jax
import jax.numpy as jnp
from jax import lax
from jax.experimental import pallas as pl
from jax.experimental.pallas import tpu as pltpu
from jax.sharding import PartitionSpec as P

BLK = 128
LAYERS = 2
ROWS = 512
PARTS = (4, 4)
AHEAD = 8
PROJECT_FLOPS = 10 * 1153 * 10**6
SECOND_FLOPS = 5 * 1153 * 10**6
MIB = 2**20
F32 = jnp.float32
BF16 = jnp.bfloat16


def dot(x, y):
    return jnp.dot(x, y, preferred_element_type=F32)


def dot_nt(x, y):
    return lax.dot_general(x, y, (((1,), (1,)), ((), ())), preferred_element_type=F32)


def hop(values, bit):
    size = lax.axis_size("src")
    return lax.ppermute(values, "src", [(i, i ^ bit) for i in range(size)])


def mirror_pairs():
    groups = lax.axis_size("tgt")
    copies = lax.axis_size("src") // groups
    pairs = []
    for p in range(groups * copies):
        a, r = divmod(p, copies)
        for q in range(groups):
            if a != q:
                pairs.append((p * groups + q, (q * copies + r) * groups + a))
    return pairs


def to_mirror(values):
    return lax.ppermute(values, ("src", "tgt"), mirror_pairs())


def call(body, name, outs, scalars, arrays, scratch=(), flops=0, limit=12):
    smem = pl.BlockSpec(memory_space=pltpu.SMEM)
    vmem = pl.BlockSpec(memory_space=pltpu.VMEM)
    return pl.pallas_call(
        body,
        in_specs=[smem] * len(scalars) + [vmem] * len(arrays),
        out_specs=[vmem] * len(outs),
        scratch_shapes=list(scratch),
        out_shape=list(outs),
        name=name,
        compiler_params=pltpu.CompilerParams(vmem_limit_bytes=limit * MIB),
        cost_estimate=pl.CostEstimate(flops=flops, bytes_accessed=0, transcendentals=0),
    )(*scalars, *arrays)


def reverse_column(reverse_row):
    return jnp.broadcast_to(reverse_row[...], (8, reverse_row.shape[1])).T[:, :1]


def own_mirror():
    copies = lax.axis_size("src") // lax.axis_size("tgt")
    return lax.axis_index("src") // copies == lax.axis_index("tgt")


def like(shape, dtype):
    return jax.ShapeDtypeStruct(shape, dtype)


def by_core(on_first, on_second):
    return jnp.where(lax.axis_index("src") % 2 == 0, on_first, on_second)


def project_body(w_proj_t, state, out, ahead, *parts):
    out[...] = dot_nt(w_proj_t[0], state[...]).astype(BF16)
    start, count = ahead.shape[0], len(parts) // 2
    half = (state.shape[0] - start) // 2
    ahead[...] = state[:start, :]
    for keep, swap in zip(parts[:count], parts[count:]):
        rows = keep.shape[0]
        low, high = state[pl.ds(start, rows), :], state[pl.ds(half + start, rows), :]
        keep[...] = by_core(low, high)
        swap[...] = by_core(high, low)
        start += rows


def project(w_proj_t, state):
    width, (edges, features) = w_proj_t.shape[1], state.shape
    ahead = edges // AHEAD
    sizes = [(edges - ahead) // 2 * part // sum(PARTS) for part in PARTS]
    outs = call(
        project_body,
        "project",
        [like((width, edges), BF16)]
        + [like((n, features), BF16) for n in [ahead] + sizes * 2],
        [],
        [w_proj_t, state],
        limit=8,
        flops=PROJECT_FLOPS,
    )
    return outs[0], outs[1], outs[2 : 2 + len(sizes)], outs[2 + len(sizes) :]


def add_blocks(index, slots, blocks, pool, add):
    mine = lax.axis_index("src")

    def one(slot, carry):
        source = index[slots + slot]
        relative = (source // blocks) ^ mine
        tile = jnp.int32(0)
        place, bit = 1, lax.axis_size("src") // 2
        while place < pool.shape[0]:
            tile = tile + jnp.where((relative & bit) != 0, place, 0)
            place, bit = place * 2, bit // 2
        start = pl.multiple_of((source % blocks) * BLK, BLK)
        into = pl.multiple_of(index[slot] * BLK, BLK)

        @pl.when((relative & 1) == 0)
        def _():
            add(slot, pool[tile, :, pl.ds(start, BLK)], into)

        return carry

    lax.fori_loop(0, jnp.minimum(index[2 * slots], slots), one, 0)


def triplet_body(blocks, own_index, other_index, pool, own_coeffs, other_coeffs, kept, sent, acc):
    acc[...] = jnp.zeros_like(acc)
    for tile, (index, coeffs) in enumerate(
        [(own_index, own_coeffs), (other_index, other_coeffs)]
    ):

        def add(slot, rows, into):
            acc[tile, :, pl.ds(into, BLK)] += dot(rows, coeffs[slot])

        add_blocks(index, coeffs.shape[0], blocks, pool, add)
    kept[...] = acc[0]
    sent[...] = acc[1].astype(BF16)


def triplet_partials(index, pool, coeffs):
    width, edges = pool.shape[1:]
    return call(
        functools.partial(triplet_body, edges // BLK),
        "triplets",
        [like((width, edges), F32), like((width, edges), BF16)],
        index,
        [pool] + coeffs,
        scratch=[pltpu.VMEM((2, width, edges), F32)],
        limit=8,
    )


def branch_of(x, agg, w_up, w_in, w_out, gain):
    summed = x.astype(F32) + dot(agg, w_up[...])
    scale_inv = lax.rsqrt(jnp.mean(summed * summed, axis=-1, keepdims=True) + 1e-06)
    normed = (gain[...] * summed * scale_inv).astype(BF16)
    u = dot(normed, w_in[...])
    activated = (u / (1.0 + jnp.exp(-u))).astype(BF16)
    return summed, dot(activated, w_out[...]).astype(BF16)


def chunks(edges):
    step = min(ROWS, edges)
    return [pl.ds(i, step) for i in range(0, edges, step)]


def weights_of(layer_index, w_up, w_in, w_out, gain):
    return [w.at[layer_index] for w in (w_up, w_in, w_out)] + [gain.at[pl.ds(layer_index, 1)]]


def picking(column, rows, edges):
    lanes = lax.broadcasted_iota(jnp.int32, (rows.size, edges), 1)
    return (column[rows.start : rows.start + rows.size] == lanes).astype(BF16)


def first_body(
    w_up, w_in, w_out, gain, w_proj_t, agg_t, reverse, state, total, branch, v_t, u_t
):
    weights = weights_of(0, w_up, w_in, w_out, gain)
    agg = agg_t[...].astype(F32).T.astype(BF16)
    w_next = w_proj_t[1]
    edges = state.shape[0]
    for rows in chunks(edges):
        summed, out = branch_of(state[rows, :], agg[rows.start : rows.start + rows.size], *weights)
        branch[rows, :] = out
        total[rows, :] = summed + out.astype(F32)
    u = dot_nt(w_next, branch[...]).astype(BF16)
    at = lax.broadcasted_iota(jnp.int32, (edges, edges), 0)
    turned = dot_nt(u, (reverse[...] == at).astype(BF16))
    v = dot_nt(w_next, total[...].astype(BF16))
    u_t[...] = turned.astype(BF16)
    v_t[...] = jnp.where(own_mirror(), v + turned, v).astype(BF16)


def combine_body(v_t, u_mirror, out):
    v = v_t[...].astype(F32)
    out[0] = jnp.where(own_mirror(), v, v + u_mirror[...].astype(F32)).astype(BF16)


def combine_pair_body(v_t, v_other, u_mirror, u_across, out):
    v, other = v_t[...].astype(F32), v_other[...].astype(F32)
    here = own_mirror()
    out[0] = jnp.where(here, v, v + u_mirror[...].astype(F32)).astype(BF16)
    out[1] = jnp.where(here, other + u_across[...].astype(F32), other).astype(BF16)


def second_body(
    w_up, w_in, w_out, gain, agg_t, agg_other, reverse, total, branch, own, *rest
):
    edges = total.shape[0]
    weights = weights_of(0, w_up, w_in, w_out, gain)
    here = own_mirror()
    *other, state, mirrored = rest
    if len(other) == 1:
        received = other[0][...]
    else:
        first, first_passed, *other = other
        count = len(other) // 2
        passed = jnp.concatenate([y[...] for y in other[count:]], axis=0)
        routed = jnp.concatenate([x[: y.shape[0], :] for x, y in zip(other, other[count:])], axis=0)
        received = jnp.concatenate(
            [
                by_core(first[: first_passed.shape[0], :], first_passed[...]),
                by_core(routed, passed),
                by_core(passed, routed),
            ],
            axis=0,
        )
    source = jnp.where(here, own[...], received)
    low = jnp.where(here, agg_t[...], agg_other[...])
    column = reverse_column(reverse)
    for rows in chunks(edges):
        pick = picking(column, rows, edges)
        summed, out = branch_of(dot(pick, source), dot_nt(pick, low).astype(BF16), *weights)
        state[rows, :] = (total[rows, :] + out.astype(F32)).astype(BF16)
        mirrored[rows, :] = (summed + out.astype(F32) + branch[rows, :].astype(F32)).astype(BF16)


def third_body(w_up, w_in, w_out, gain, state, agg_t, total):
    weights = weights_of(1, w_up, w_in, w_out, gain)
    agg = agg_t[...].astype(F32).T.astype(BF16)
    for rows in chunks(state.shape[0]):
        summed, out = branch_of(state[rows, :], agg[rows.start : rows.start + rows.size], *weights)
        total[rows, :] = summed + out.astype(F32)


def last_body(w_up, w_in, w_out, gain, mirrored, agg_t, agg_other, reverse, total, state):
    edges = total.shape[0]
    weights = weights_of(1, w_up, w_in, w_out, gain)
    low = jnp.where(own_mirror(), agg_t[...], agg_other[...])
    at = lax.broadcasted_iota(jnp.int32, (edges, edges), 0)
    agg = dot(low, (reverse[...] == at).astype(BF16)).T.astype(BF16)
    for rows in chunks(edges):
        summed, out = branch_of(
            mirrored[rows, :], agg[rows.start : rows.start + rows.size], *weights
        )
        state[rows, :] = (total[rows, :] + out.astype(F32)).astype(BF16)


def gather_step(held, bit):
    return jnp.concatenate([held, hop(held, bit)], axis=0)


def stage_routes(keep, swap):
    message = jnp.concatenate([keep, hop(swap, 1)], axis=0)
    copies = lax.axis_size("src") // 2
    pairs = []
    for a in range(2):
        for r in range(copies):
            row = (a * copies + r) * 2
            pairs += [(row + 1 - a, row + a)] if r % 2 else [(row, row), (row + 1, row + 1)]
    return lax.ppermute(message, ("src", "tgt"), pairs)


def send_routes(staged):
    copies = lax.axis_size("src") // 2
    pairs = []
    for a in range(2):
        for r in range(copies):
            across = (1 - a) * copies + r
            if r % 2:
                pairs.append(((a * copies + r) * 2 + a, across * 2 + a))
            else:
                pairs.append(((a * copies + r) * 2 + 1 - a, across * 2 + a))
    return lax.ppermute(staged, ("src", "tgt"), pairs)


def send_ahead(rows):
    copies = lax.axis_size("src") // 2
    pairs = [
        ((a * copies + r) * 2 + 1 - a, ((1 - a) * copies + r) * 2 + a)
        for a in range(2)
        for r in range(0, copies, 2)
    ]
    return lax.ppermute(jnp.concatenate([rows, hop(rows, 1)], axis=0), ("src", "tgt"), pairs)


def pass_on(routed):
    return hop(routed[routed.shape[0] // 2 :], 1)


def gather_down(held, last):
    bit = lax.axis_size("src") // 2 // held.shape[0]
    while bit >= last:
        held = gather_step(held, bit)
        bit //= 2
    return held


def next_pool(v_t, u_t):
    size, groups = lax.axis_size("src"), lax.axis_size("tgt")
    u_mirror = to_mirror(u_t)
    if groups != 2:
        return call(combine_body, "combine", [like((1,) + v_t.shape, BF16)], [], [v_t, u_mirror])[0]
    v_other = hop(v_t, size // 2)
    copies = size // 2
    pairs = [
        ((a * copies + r) * 2 + 1 - a, (a * copies + r) * 2 + a)
        for a in range(2)
        for r in range(copies)
    ]
    u_across = lax.ppermute(u_t, ("src", "tgt"), pairs)
    return call(
        combine_pair_body,
        "combine",
        [like((2,) + v_t.shape, BF16)],
        [],
        [v_t, v_other, u_mirror, u_across],
        limit=4,
    )[0]


def sum_over_cores(kept, sent):
    return (kept + hop(sent, 1).astype(F32)).astype(BF16)


def local(
    edge_states,
    triplet_coeff,
    block_target,
    block_source,
    block_count,
    reverse_slot,
    w_proj,
    w_up,
    w_in,
    w_out,
    norm_gain,
):
    state0 = edge_states[0, 0]
    edges, features = state0.shape
    width = w_proj.shape[2]
    reverse = reverse_slot[0]
    w_proj_t = jnp.swapaxes(w_proj, 1, 2)
    weights = [w_up, w_in, w_out, norm_gain]

    own_index = jnp.concatenate([block_target[0, 0], block_source[0, 0], block_count[0]])
    own_coeffs = triplet_coeff[0, 0]
    index, coeffs = [own_index, hop(own_index, 1)], [own_coeffs, hop(own_coeffs, 1)]
    paired = lax.axis_size("tgt") == 2
    proj0, ahead, keep, swap = project(w_proj_t, state0)
    if paired:
        staged = [stage_routes(x, y) for x, y in zip(keep, swap)]
    else:
        staged = [state0]
    pool = gather_down(proj0[None], 4)
    first = [send_ahead(ahead)] if paired else []
    index, coeffs, first, pool = lax.optimization_barrier((index, coeffs, first, pool))
    first += [pass_on(x) for x in first]
    routed = [send_routes(x) if paired else to_mirror(x) for x in staged]
    agg0 = sum_over_cores(*triplet_partials(index, gather_down(pool, 2), coeffs))
    total0, branch0, v_t, u_t = call(
        first_body,
        "first",
        [
            like((edges, features), F32),
            like((edges, features), BF16),
            like((width, edges), BF16),
            like((width, edges), BF16),
        ],
        [],
        weights + [w_proj_t, agg0, reverse, state0],
    )
    passed = [pass_on(routed[0])] if paired else []
    u_t, v_t, routed, passed = lax.optimization_barrier((u_t, v_t, routed, passed))
    held1 = next_pool(v_t, u_t)
    routed, agg0_sent, held1 = lax.optimization_barrier((routed, agg0, held1))
    received = first + routed + passed + [pass_on(x) for x in routed[1:] if paired]
    agg0_other = to_mirror(agg0_sent)
    pool1 = gather_down(held1, 4)
    near1 = gather_down(pool1, 2)
    state1, mirrored1 = call(
        second_body,
        "second",
        [like((edges, features), BF16), like((edges, features), BF16)],
        [],
        weights
        + [agg0, agg0_other, reverse, total0, branch0, state0]
        + received,
        flops=SECOND_FLOPS,
    )
    near1, state1, mirrored1 = lax.optimization_barrier((near1, state1, mirrored1))
    kept, sent = triplet_partials(index, near1, coeffs)
    agg1 = sum_over_cores(kept, sent)
    agg1_other = to_mirror(agg1)
    total1 = call(
        third_body,
        "third",
        [like((edges, features), F32)],
        [],
        weights + [state1, agg1],
    )[0]
    final = call(
        last_body,
        "last",
        [like((edges, features), BF16)],
        [],
        weights + [mirrored1, agg1, agg1_other, reverse, total1],
    )[0]
    return final[None, None]


def solution(mesh):
    return jax.shard_map(
        local,
        mesh=mesh,
        in_specs=(
            P("src", "tgt", None, None),
            P("src", "tgt", None, None, None),
            P("src", "tgt", None),
            P("src", "tgt", None),
            P("src", "tgt"),
            P("src", "tgt", None),
            P(),
            P(),
            P(),
            P(),
            P(),
        ),
        out_specs=P("src", "tgt", None, None),
        check_vma=False,
    )
```

```python
import functools

import jax
import jax.numpy as jnp
from jax import lax
from jax.experimental import pallas as pl
from jax.experimental.pallas import tpu as pltpu
from jax.sharding import PartitionSpec as P

BLK = 128
LAYERS = 2
ROWS = 512
PARTS = (4, 4)
AHEAD = 8
PROJECT_FLOPS = 10 * 1153 * 10**6
SECOND_FLOPS = 5 * 1153 * 10**6
MIB = 2**20
F32 = jnp.float32
BF16 = jnp.bfloat16


def dot(x, y):
    return jnp.dot(x, y, preferred_element_type=F32)


def dot_nt(x, y):
    return lax.dot_general(x, y, (((1,), (1,)), ((), ())), preferred_element_type=F32)


def hop(values, bit):
    size = lax.axis_size("src")
    return lax.ppermute(values, "src", [(i, i ^ bit) for i in range(size)])


def mirror_pairs():
    groups = lax.axis_size("tgt")
    copies = lax.axis_size("src") // groups
    pairs = []
    for p in range(groups * copies):
        a, r = divmod(p, copies)
        for q in range(groups):
            if a != q:
                pairs.append((p * groups + q, (q * copies + r) * groups + a))
    return pairs


def to_mirror(values):
    return lax.ppermute(values, ("src", "tgt"), mirror_pairs())


def call(body, name, outs, scalars, arrays, scratch=(), flops=0, limit=12):
    smem = pl.BlockSpec(memory_space=pltpu.SMEM)
    vmem = pl.BlockSpec(memory_space=pltpu.VMEM)
    return pl.pallas_call(
        body,
        in_specs=[smem] * len(scalars) + [vmem] * len(arrays),
        out_specs=[vmem] * len(outs),
        scratch_shapes=list(scratch),
        out_shape=list(outs),
        name=name,
        compiler_params=pltpu.CompilerParams(vmem_limit_bytes=limit * MIB),
        cost_estimate=pl.CostEstimate(flops=flops, bytes_accessed=0, transcendentals=0),
    )(*scalars, *arrays)


def reverse_column(reverse_row):
    return jnp.broadcast_to(reverse_row[...], (8, reverse_row.shape[1])).T[:, :1]


def own_mirror():
    copies = lax.axis_size("src") // lax.axis_size("tgt")
    return lax.axis_index("src") // copies == lax.axis_index("tgt")


def like(shape, dtype):
    return jax.ShapeDtypeStruct(shape, dtype)


def by_core(on_first, on_second):
    return jnp.where(lax.axis_index("src") % 2 == 0, on_first, on_second)


def project_body(w_proj_t, state, out, ahead, *parts):
    out[...] = dot_nt(w_proj_t[0], state[...]).astype(BF16)
    start, count = ahead.shape[0], len(parts) // 2
    half = (state.shape[0] - start) // 2
    ahead[...] = state[:start, :]
    for keep, swap in zip(parts[:count], parts[count:]):
        rows = keep.shape[0]
        low, high = state[pl.ds(start, rows), :], state[pl.ds(half + start, rows), :]
        keep[...] = by_core(low, high)
        swap[...] = by_core(high, low)
        start += rows


def project(w_proj_t, state):
    width, (edges, features) = w_proj_t.shape[1], state.shape
    ahead = edges // AHEAD
    sizes = [(edges - ahead) // 2 * part // sum(PARTS) for part in PARTS]
    outs = call(
        project_body,
        "project",
        [like((width, edges), BF16)]
        + [like((n, features), BF16) for n in [ahead] + sizes * 2],
        [],
        [w_proj_t, state],
        limit=8,
        flops=PROJECT_FLOPS,
    )
    return outs[0], outs[1], outs[2 : 2 + len(sizes)], outs[2 + len(sizes) :]


def add_blocks(index, slots, blocks, pool, add):
    mine = lax.axis_index("src")

    def one(slot, carry):
        source = index[slots + slot]
        relative = (source // blocks) ^ mine
        tile = jnp.int32(0)
        place, bit = 1, lax.axis_size("src") // 2
        while place < pool.shape[0]:
            tile = tile + jnp.where((relative & bit) != 0, place, 0)
            place, bit = place * 2, bit // 2
        start = pl.multiple_of((source % blocks) * BLK, BLK)
        into = pl.multiple_of(index[slot] * BLK, BLK)

        @pl.when((relative & 1) == 0)
        def _():
            add(slot, pool[tile, :, pl.ds(start, BLK)], into)

        return carry

    lax.fori_loop(0, jnp.minimum(index[2 * slots], slots), one, 0)


def triplet_body(blocks, own_index, other_index, pool, own_coeffs, other_coeffs, kept, sent, acc):
    acc[...] = jnp.zeros_like(acc)
    for tile, (index, coeffs) in enumerate(
        [(own_index, own_coeffs), (other_index, other_coeffs)]
    ):

        def add(slot, rows, into):
            acc[tile, :, pl.ds(into, BLK)] += dot(rows, coeffs[slot])

        add_blocks(index, coeffs.shape[0], blocks, pool, add)
    kept[...] = acc[0]
    sent[...] = acc[1].astype(BF16)


def triplet_partials(index, pool, coeffs):
    width, edges = pool.shape[1:]
    return call(
        functools.partial(triplet_body, edges // BLK),
        "triplets",
        [like((width, edges), F32), like((width, edges), BF16)],
        index,
        [pool] + coeffs,
        scratch=[pltpu.VMEM((2, width, edges), F32)],
        limit=8,
    )


def branch_of(x, agg, w_up, w_in, w_out, gain):
    summed = x.astype(F32) + dot(agg, w_up[...])
    scale_inv = lax.rsqrt(jnp.mean(summed * summed, axis=-1, keepdims=True) + 1e-06)
    normed = (gain[...] * summed * scale_inv).astype(BF16)
    u = dot(normed, w_in[...])
    activated = (u / (1.0 + jnp.exp(-u))).astype(BF16)
    return summed, dot(activated, w_out[...]).astype(BF16)


def chunks(edges):
    step = min(ROWS, edges)
    return [pl.ds(i, step) for i in range(0, edges, step)]


def weights_of(layer_index, w_up, w_in, w_out, gain):
    return [w.at[layer_index] for w in (w_up, w_in, w_out)] + [gain.at[pl.ds(layer_index, 1)]]


def picking(column, rows, edges):
    lanes = lax.broadcasted_iota(jnp.int32, (rows.size, edges), 1)
    return (column[rows.start : rows.start + rows.size] == lanes).astype(BF16)


def first_body(
    w_up, w_in, w_out, gain, w_proj_t, agg_t, reverse, state, total, branch, v_t, u_t
):
    weights = weights_of(0, w_up, w_in, w_out, gain)
    agg = agg_t[...].astype(F32).T.astype(BF16)
    w_next = w_proj_t[1]
    edges = state.shape[0]
    for rows in chunks(edges):
        summed, out = branch_of(state[rows, :], agg[rows.start : rows.start + rows.size], *weights)
        branch[rows, :] = out
        total[rows, :] = summed + out.astype(F32)
    u = dot_nt(w_next, branch[...]).astype(BF16)
    at = lax.broadcasted_iota(jnp.int32, (edges, edges), 0)
    turned = dot_nt(u, (reverse[...] == at).astype(BF16))
    v = dot_nt(w_next, total[...].astype(BF16))
    u_t[...] = turned.astype(BF16)
    v_t[...] = jnp.where(own_mirror(), v + turned, v).astype(BF16)


def combine_body(v_t, u_mirror, out):
    v = v_t[...].astype(F32)
    out[0] = jnp.where(own_mirror(), v, v + u_mirror[...].astype(F32)).astype(BF16)


def combine_pair_body(v_t, v_other, u_mirror, u_across, out):
    v, other = v_t[...].astype(F32), v_other[...].astype(F32)
    here = own_mirror()
    out[0] = jnp.where(here, v, v + u_mirror[...].astype(F32)).astype(BF16)
    out[1] = jnp.where(here, other + u_across[...].astype(F32), other).astype(BF16)


def second_body(
    w_up, w_in, w_out, gain, agg_t, agg_other, reverse, total, branch, own, *rest
):
    edges = total.shape[0]
    weights = weights_of(0, w_up, w_in, w_out, gain)
    here = own_mirror()
    *other, state, mirrored = rest
    if len(other) == 1:
        received = other[0][...]
    else:
        first, first_passed, *other = other
        count = len(other) // 2
        passed = jnp.concatenate([y[...] for y in other[count:]], axis=0)
        routed = jnp.concatenate([x[: y.shape[0], :] for x, y in zip(other, other[count:])], axis=0)
        received = jnp.concatenate(
            [
                by_core(first[: first_passed.shape[0], :], first_passed[...]),
                by_core(routed, passed),
                by_core(passed, routed),
            ],
            axis=0,
        )
    source = jnp.where(here, own[...], received)
    low = jnp.where(here, agg_t[...], agg_other[...])
    column = reverse_column(reverse)
    for rows in chunks(edges):
        pick = picking(column, rows, edges)
        summed, out = branch_of(dot(pick, source), dot_nt(pick, low).astype(BF16), *weights)
        state[rows, :] = (total[rows, :] + out.astype(F32)).astype(BF16)
        mirrored[rows, :] = (summed + out.astype(F32) + branch[rows, :].astype(F32)).astype(BF16)


def third_body(w_up, w_in, w_out, gain, state, agg_t, total):
    weights = weights_of(1, w_up, w_in, w_out, gain)
    agg = agg_t[...].astype(F32).T.astype(BF16)
    for rows in chunks(state.shape[0]):
        summed, out = branch_of(state[rows, :], agg[rows.start : rows.start + rows.size], *weights)
        total[rows, :] = summed + out.astype(F32)


def last_body(w_up, w_in, w_out, gain, mirrored, agg_t, agg_other, reverse, total, state):
    edges = total.shape[0]
    weights = weights_of(1, w_up, w_in, w_out, gain)
    low = jnp.where(own_mirror(), agg_t[...], agg_other[...])
    at = lax.broadcasted_iota(jnp.int32, (edges, edges), 0)
    agg = dot(low, (reverse[...] == at).astype(BF16)).T.astype(BF16)
    for rows in chunks(edges):
        summed, out = branch_of(
            mirrored[rows, :], agg[rows.start : rows.start + rows.size], *weights
        )
        state[rows, :] = (total[rows, :] + out.astype(F32)).astype(BF16)


def gather_step(held, bit):
    return jnp.concatenate([held, hop(held, bit)], axis=0)


def stage_routes(keep, swap):
    message = jnp.concatenate([keep, hop(swap, 1)], axis=0)
    copies = lax.axis_size("src") // 2
    pairs = []
    for a in range(2):
        for r in range(copies):
            row = (a * copies + r) * 2
            pairs += [(row + 1 - a, row + a)] if r % 2 else [(row, row), (row + 1, row + 1)]
    return lax.ppermute(message, ("src", "tgt"), pairs)


def send_routes(staged):
    copies = lax.axis_size("src") // 2
    pairs = []
    for a in range(2):
        for r in range(copies):
            across = (1 - a) * copies + r
            if r % 2:
                pairs.append(((a * copies + r) * 2 + a, across * 2 + a))
            else:
                pairs.append(((a * copies + r) * 2 + 1 - a, across * 2 + a))
    return lax.ppermute(staged, ("src", "tgt"), pairs)


def send_ahead(rows):
    copies = lax.axis_size("src") // 2
    pairs = [
        ((a * copies + r) * 2 + 1 - a, ((1 - a) * copies + r) * 2 + a)
        for a in range(2)
        for r in range(0, copies, 2)
    ]
    return lax.ppermute(jnp.concatenate([rows, hop(rows, 1)], axis=0), ("src", "tgt"), pairs)


def pass_on(routed):
    return hop(routed[routed.shape[0] // 2 :], 1)


def gather_down(held, last):
    bit = lax.axis_size("src") // 2 // held.shape[0]
    while bit >= last:
        held = gather_step(held, bit)
        bit //= 2
    return held


def next_pool(v_t, u_t):
    size, groups = lax.axis_size("src"), lax.axis_size("tgt")
    u_mirror = to_mirror(u_t)
    if groups != 2:
        return call(combine_body, "combine", [like((1,) + v_t.shape, BF16)], [], [v_t, u_mirror])[0]
    v_other = hop(v_t, size // 2)
    copies = size // 2
    pairs = [
        ((a * copies + r) * 2 + 1 - a, (a * copies + r) * 2 + a)
        for a in range(2)
        for r in range(copies)
    ]
    u_across = lax.ppermute(u_t, ("src", "tgt"), pairs)
    return call(
        combine_pair_body,
        "combine",
        [like((2,) + v_t.shape, BF16)],
        [],
        [v_t, v_other, u_mirror, u_across],
        limit=4,
    )[0]


def sum_over_cores(kept, sent):
    return (kept + hop(sent, 1).astype(F32)).astype(BF16)


def local(
    edge_states,
    triplet_coeff,
    block_target,
    block_source,
    block_count,
    reverse_slot,
    w_proj,
    w_up,
    w_in,
    w_out,
    norm_gain,
):
    state0 = edge_states[0, 0]
    edges, features = state0.shape
    width = w_proj.shape[2]
    reverse = reverse_slot[0]
    w_proj_t = jnp.swapaxes(w_proj, 1, 2)
    weights = [w_up, w_in, w_out, norm_gain]

    own_index = jnp.concatenate([block_target[0, 0], block_source[0, 0], block_count[0]])
    own_coeffs = triplet_coeff[0, 0]
    paired = lax.axis_size("tgt") == 2
    proj0, ahead, keep, swap = project(w_proj_t, state0)
    if paired:
        staged = [stage_routes(x, y) for x, y in zip(keep, swap)]
    else:
        staged = [state0]
    pool = gather_down(proj0[None], 4)
    first = [send_ahead(ahead)] if paired else []
    own_index, own_coeffs, first, pool = lax.optimization_barrier(
        (own_index, own_coeffs, first, pool)
    )
    index, coeffs = [own_index, hop(own_index, 1)], [own_coeffs, hop(own_coeffs, 1)]
    first += [pass_on(x) for x in first]
    routed = [send_routes(x) if paired else to_mirror(x) for x in staged]
    agg0 = sum_over_cores(*triplet_partials(index, gather_down(pool, 2), coeffs))
    total0, branch0, v_t, u_t = call(
        first_body,
        "first",
        [
            like((edges, features), F32),
            like((edges, features), BF16),
            like((width, edges), BF16),
            like((width, edges), BF16),
        ],
        [],
        weights + [w_proj_t, agg0, reverse, state0],
    )
    passed = [pass_on(routed[0])] if paired else []
    u_t, v_t, routed, passed = lax.optimization_barrier((u_t, v_t, routed, passed))
    held1 = next_pool(v_t, u_t)
    routed, agg0_sent, held1 = lax.optimization_barrier((routed, agg0, held1))
    received = first + routed + passed + [pass_on(x) for x in routed[1:] if paired]
    agg0_other = to_mirror(agg0_sent)
    pool1 = gather_down(held1, 4)
    near1 = gather_down(pool1, 2)
    state1, mirrored1 = call(
        second_body,
        "second",
        [like((edges, features), BF16), like((edges, features), BF16)],
        [],
        weights
        + [agg0, agg0_other, reverse, total0, branch0, state0]
        + received,
        flops=SECOND_FLOPS,
    )
    near1, state1, mirrored1 = lax.optimization_barrier((near1, state1, mirrored1))
    kept, sent = triplet_partials(index, near1, coeffs)
    agg1 = sum_over_cores(kept, sent)
    agg1_other = to_mirror(agg1)
    total1 = call(
        third_body,
        "third",
        [like((edges, features), F32)],
        [],
        weights + [state1, agg1],
    )[0]
    final = call(
        last_body,
        "last",
        [like((edges, features), BF16)],
        [],
        weights + [mirrored1, agg1, agg1_other, reverse, total1],
    )[0]
    return final[None, None]


def solution(mesh):
    return jax.shard_map(
        local,
        mesh=mesh,
        in_specs=(
            P("src", "tgt", None, None),
            P("src", "tgt", None, None, None),
            P("src", "tgt", None),
            P("src", "tgt", None),
            P("src", "tgt"),
            P("src", "tgt", None),
            P(),
            P(),
            P(),
            P(),
            P(),
        ),
        out_specs=P("src", "tgt", None, None),
        check_vma=False,
    )
```
